1024 devices in a mesh: gz: 32 (over z_hi, y), gx: 32 (over x, z_lo, core).
Axes of the slice: x: 4, y: 8, z: 16 (z_hi: 4, z_lo: 4; z = z_hi * 4 + z_lo), core: 2. Of those that a mesh axis runs over, the one named last changes fastest.
Arguments:
- phase_field: float32 [256, 1024, 1024], P('gz', 'gx'), may hold values from -1 to 1
- solute: float32 [256, 1024, 1024], P('gz', 'gx'), may hold values from -1 to 0.5
- pull_counts: int32 [2], replicated, may hold values from 1 to 5, as said below
- planes: int32 [32], P('gz'), may hold values from 0 to 255, as said below
Outputs:
- final_phase: float32 [256, 1024, 1024], P('gz', 'gx')
- correlation: float32 [32, 1024, 1024], P('gz', 'gx')
The draws below stay inside these ranges and needn't reach their ends.
Inputs may be any that keep to these rules, and one draw needn't show every extreme that they name: `pull_counts`: 5 occurs. `planes`: entry s lies between 8 s and 8 s + 7.
All inputs are finite; a program needn't handle non-finite values.
Results may differ from the reference program's by a relative error of at most 0.00021.
Values sent between devices are 32-bit elements; how exact they have to be, the bound alone decides.
A program may use at most 32 MiB of HBM per device.

```python
import math
from functools import partial
import jax
import jax.numpy as jnp
from jax import lax

NY = 1024
STEPS = 2
PMAX = 5
EVERY = 8
NX = 1024
NZ = 256
NS = 32


def draw_pull_counts(key, part):
    key = jax.random.fold_in(key, 11)
    counts = jax.random.randint(jax.random.fold_in(key, 1), (STEPS,), 1, PMAX + 1)
    where_most = jax.random.randint(jax.random.fold_in(key, 2), (), 0, STEPS)
    counts = jnp.where(jnp.arange(STEPS, dtype=jnp.int32) == where_most, PMAX, counts)
    return counts.astype(jnp.int32)


def draw_planes(key, part):
    offsets = jax.random.randint(jax.random.fold_in(key, 21), (NS,), 0, EVERY)
    ordering = jax.random.permutation(jax.random.fold_in(key, 22), NS)
    offsets = offsets.at[ordering[0]].set(0).at[ordering[1]].set(EVERY - 1)
    return (jnp.arange(NS, dtype=jnp.int32) * EVERY + offsets).astype(jnp.int32)


def level_of(stream_key, shape, shards, least, largest):
    factor_of = 1.0
    for position, blocks in shards:
        steps = jax.random.uniform(jax.random.fold_in(jax.random.fold_in(stream_key, 6), position), (blocks,), jnp.float32, least / len(shards), largest / len(shards))
        factor_of = factor_of * jnp.repeat(jnp.exp(steps), shape[position] // blocks).reshape((-1,) + (1,) * (len(shape) - 1 - position))
    return factor_of


def setup_inputs(seed: int = 0) -> dict:
    key_list = jax.random.split(jax.random.key(seed), 5)
    return {
        "phase_field": jnp.clip(jax.random.uniform(key_list[0], (NZ, NX, NY), jnp.float32, -1.0, 1.0) * level_of(key_list[0], (NZ, NX, NY), ((0, 32), (1, 32)), -0.4, 0.0), -1.0, 1.0),
        "solute": jnp.clip(-1.0 + 1.5 * jax.random.uniform(key_list[1], (NZ, NX, NY), jnp.float32) ** level_of(key_list[1], (NZ, NX, NY), ((0, 32), (1, 32)), -0.2, 0.2), -1.0, 0.5),
        "pull_counts": draw_pull_counts(jax.random.fold_in(key_list[4], 71), 0),
        "planes": draw_planes(jax.random.fold_in(key_list[4], 71), 0),
    }


TIME_STEP = 0.05
PARTITION = 0.15
COUPLING = 1.6
DIFFUSIVITY = 0.4
FAR_FIELD = -1.0
BLOCK_ROWS = 8

def pull_frame(field, pull_now):
    far_planes = jnp.full((PMAX,) + field.shape[1:], FAR_FIELD, field.dtype)
    widened = jnp.concatenate([field, far_planes], 0)
    return lax.dynamic_slice_in_dim(widened, pull_now, field.shape[0], 0)

def advance(phase_now, solute_now, with_solute):
    phase_pad = jnp.concatenate([phase_now[:1], phase_now, phase_now[-1:]], 0)
    solute_pad = jnp.concatenate([solute_now[:1], solute_now, solute_now[-1:]], 0)

    def update(first_row):
        phase_rows = lax.dynamic_slice_in_dim(phase_pad, first_row, BLOCK_ROWS + 2, 0)
        solute_rows = lax.dynamic_slice_in_dim(solute_pad, first_row, BLOCK_ROWS + 2, 0)
        centre = phase_rows[1:-1]
        solute_here = solute_rows[1:-1]
        phase_sides = [phase_rows[:-2], phase_rows[2:], jnp.roll(centre, 1, 1), jnp.roll(centre, -1, 1), jnp.roll(centre, 1, 2), jnp.roll(centre, -1, 2)]
        heights = (first_row + jnp.arange(BLOCK_ROWS, dtype=jnp.int32)).astype(jnp.float32)
        thermal = ((2.0 * heights - NZ) / NZ)[:, None, None]
        laplace = sum(phase_sides) - 6.0 * centre
        driving = laplace + centre - centre * centre * centre - COUPLING * (1.0 - centre * centre) * (1.0 - centre * centre) * (solute_here + thermal)
        phase_next = jnp.clip(centre + TIME_STEP * driving, -1.0, 1.0)
        if not with_solute:
            return (phase_next, solute_here)
        solute_sides = [solute_rows[:-2], solute_rows[2:], jnp.roll(solute_here, 1, 1), jnp.roll(solute_here, -1, 1), jnp.roll(solute_here, 1, 2), jnp.roll(solute_here, -1, 2)]
        mobility = 0.5 * (1.0 - centre)
        solute_flux = sum((0.5 * (mobility + 0.5 * (1.0 - phase_side)) * (solute_side - solute_here) for phase_side, solute_side in zip(phase_sides, solute_sides)))
        solute_rate = (DIFFUSIVITY * solute_flux + 0.5 * (1.0 + (1.0 - PARTITION) * solute_here) * driving) / (0.5 * (1.0 + PARTITION) - 0.5 * (1.0 - PARTITION) * centre)
        return (phase_next, solute_here + TIME_STEP * solute_rate)
    starts = jnp.arange(NZ // BLOCK_ROWS, dtype=jnp.int32) * BLOCK_ROWS
    phase_blocks, solute_blocks = lax.map(update, starts)
    return (phase_blocks.reshape(phase_now.shape), solute_blocks.reshape(solute_now.shape))

def correlate(phase_now, plane_index):
    section = lax.dynamic_index_in_dim(phase_now, plane_index, 0, keepdims=False)
    fluctuation = section - jnp.mean(section)
    spectrum = jnp.fft.fft2(fluctuation)
    spectral_power = spectrum.real * spectrum.real + spectrum.imag * spectrum.imag
    return jnp.fft.ifft2(spectral_power).real / math.sqrt(NX * NY)

def reference(phase_field, solute, pull_counts, planes):
    phase_now, solute_now = (phase_field, solute)
    for step_index in range(STEPS):
        pull_now = pull_counts[step_index]
        phase_now = pull_frame(phase_now, pull_now)
        solute_now = pull_frame(solute_now, pull_now)
        phase_now, solute_now = advance(phase_now, solute_now, step_index < STEPS - 1)
    correlation = lax.map(partial(correlate, phase_now), planes)
    return (phase_now, correlation)
```

```python
import functools
import math

import jax
import jax.numpy as jnp
import ml_dtypes
import numpy as np
from jax import lax
from jax.experimental import pallas as pl
from jax.experimental.pallas import tpu as pltpu
from jax.sharding import PartitionSpec as P

MESH = pl.DeviceIdType.MESH
F32 = jnp.float32
BF16 = jnp.bfloat16

TIME_STEP = 0.05
PARTITION = 0.15
COUPLING = 1.6
DIFFUSIVITY = 0.4
FAR = -1.0

NP, NR, NL = 8, 32, 1024
HALF = NL // 2
RUN = 8
TOP = 8
PIECE = (8, 128)


def split_bf16(table):
    high = table.astype(ml_dtypes.bfloat16)
    low = (table - high.astype(np.float64)).astype(ml_dtypes.bfloat16)
    return np.stack([high, low])


@functools.lru_cache(None)
def tables():
    w = 2.0 * math.pi / NL
    parts, part_rows = 16, 32
    m = np.arange(parts)[:, None]
    l = np.arange(part_rows)[None, :]
    order = np.arange(HALF)
    near = np.arange(HALF)

    def trig(a, b):
        angle = (a[:, None] * b[None, :]) % NL
        return np.cos(w * angle), np.sin(w * angle)

    w1, w2 = [], []
    for odd in (0, 1):
        ky = np.broadcast_to(2 * (16 * m + l % 16) + odd, (parts, part_rows)).reshape(-1)
        imag = np.broadcast_to(l >= 16, (parts, part_rows)).reshape(-1)
        c, s = trig(near, ky)
        fwd = np.where(imag[None, :], -s, c)
        inv = 2.0 * np.where(imag[None, :], -s, c)
        if not odd:
            fwd[:, 16] = (-1.0) ** near
            inv[:, 0] = 1.0
            inv[:, 16] = (-1.0) ** near
        w1.append(fwd)
        inv = inv.reshape(HALF, parts, 4, 8).transpose(0, 2, 1, 3).reshape(HALF, HALF)
        w2.append(inv.T / (NL * NL * float(NL)))
    g, i, r = np.meshgrid(np.arange(4), np.arange(parts), np.arange(8), indexing="ij")
    x = (32 * i + 8 * g + r).reshape(-1)
    cs, back = [], []
    for odd in (0, 1):
        kx = 2 * order + odd
        cs.append(np.concatenate(trig(x, kx), 1))
        back.append(np.concatenate(trig(kx, near), 1))
    return tuple(split_bf16(np.stack(t)) for t in (w1, cs, back, w2))


def mm(x, table, odd):
    rows = x.shape[0]
    high = x.astype(BF16)
    low = (x - high.astype(F32)).astype(BF16)
    both = jnp.concatenate([high, low], 0)
    first = jnp.dot(both, table[0, odd], preferred_element_type=F32)
    second = jnp.dot(high, table[1, odd], preferred_element_type=F32)
    return first[:rows] + first[rows:] + second


def pack(block, out):
    lane_group = lax.broadcasted_iota(jnp.int32, PIECE, 1) // 32
    for c in range(8):
        v = [block[8 * g : 8 * g + 8, 128 * c : 128 * c + 128] for g in range(4)]
        for b in range(4):
            tile = v[b]
            for g in range(4):
                if g != b:
                    moved = pltpu.roll(v[g], (32 * (g - b)) % 128, 1)
                    tile = jnp.where(lane_group == g, moved, tile)
            if b:
                pass
            out[4 * c + b] = tile


def unpack(tiles):
    flat = tiles[...].reshape(256, 128)
    turned = flat.T
    return jnp.concatenate([turned[32 * g : 32 * g + 32] for g in range(4)], 1)


def seam_columns(run):
    return (0, run - 1, run // 2 - 1, run // 2)


class Message:
    def __init__(self, env, index, up, src, dst):
        self.src, self.dst, self.up = src, dst, up
        self.sems = [env["msem"].at[index, j] for j in range(4)]
        self.relay_ref = env["ra"][index]
        self.run, self.height = env["run"], env["height"]
        self.y = (self.run - 1 - env["y"]) if up else env["y"]
        self.h = (self.height - 1 - env["h"]) if up else env["h"]
        self.columns = seam_columns(self.run)

    def copy(self, src, dst, send, recv, y, h):
        if self.up:
            y, h = self.run - 1 - y, self.height - 1 - h
        return pltpu.make_async_remote_copy(
            src_ref=src,
            dst_ref=dst,
            send_sem=self.sems[send],
            recv_sem=self.sems[recv],
            device_id={"gz": h * self.run + y},
            device_id_type=MESH,
        )

    def rows(self, ref, g):
        return ref.at[:, 8 * g : 8 * g + 8, :]

    def has_target(self):
        return jnp.logical_or(self.y > 0, self.h > 0)

    def has_source(self):
        return jnp.logical_or(self.y < self.run - 1, self.h < self.height - 1)

    def start(self):
        self.start_seam()
        self.start_inside()

    def start_inside(self):
        @pl.when(self.y > 0)
        def _():
            self.copy(self.src, self.dst, 0, 1, self.y - 1, self.h).start()

    def start_seam(self):
        @pl.when(jnp.logical_and(self.y == 0, self.h > 0))
        def _():
            for g in (2, 3, 1):
                column = self.columns[g]
                self.copy(self.rows(self.src, g), self.relay_ref, 0, 3, column, self.h).start()
            end = self.run - 1
            self.copy(self.rows(self.src, 0), self.rows(self.dst, 0), 0, 1, end, self.h - 1).start()

    def relay(self, groups=(1, 2, 3)):
        end = self.run - 1
        for g in groups:

            @pl.when(jnp.logical_and(self.h > 0, self.y == self.columns[g]))
            def _(g=g):
                self.copy(self.relay_ref, self.relay_ref, 2, 3, end, self.h - 1).wait_recv()
                there = self.rows(self.dst, g)
                self.copy(self.relay_ref, there, 2, 1, end, self.h - 1).start()

    def arrive(self):
        @pl.when(self.has_source())
        def _():
            self.copy(self.src, self.dst, 0, 1, 0, 0).wait_recv()

    def finish(self):
        @pl.when(self.has_target())
        def _():
            self.copy(self.src, self.dst, 0, 1, 0, 0).wait_send()

        column = [self.y == self.columns[g] for g in (1, 2, 3)]

        @pl.when(jnp.logical_and(self.h > 0, functools.reduce(jnp.logical_or, column)))
        def _():
            self.copy(self.relay_ref, self.relay_ref, 2, 3, 0, 0).wait_send()


MESSAGES = (3, 3, 1, 1, 2, 4, 2, 2)


def lane_sides(v):
    return pltpu.roll(v, 1, 1), pltpu.roll(v, NL - 1, 1)


def driving_of(centre, total, solute_now, thermal):
    gap = 1.0 - centre * centre
    return (total - 6.0 * centre) + centre * gap - COUPLING * (gap * gap) * (solute_now + thermal)


def advance_phase(centre, driving):
    return jnp.clip(centre + TIME_STEP * driving, -1.0, 1.0)


NAMES = (
    "pulls", "plane", "phase", "solute", "w1", "cs", "back", "w2", "final", "corr", "ph", "so",
    "p1", "s1", "fb", "hsd", "hsu", "hrd", "hru", "xsl", "xsh", "xrl", "xrh", "cse", "csu",
    "cre", "cru", "ixs", "ixa", "ixb", "c2s", "c2r", "c1s", "c1r", "sd1", "rv1", "sd2", "rv2",
    "v1", "vcs", "vback", "v2",
    *["ra%d" % n for n in range(8)],
    "msem", "osem", "lsem",
)


def kernel(run, with_corr, *refs):
    r = dict(zip(NAMES, refs, strict=True))
    k = lax.axis_index("gz")
    i = lax.axis_index("gx")
    count_z, count_x = lax.axis_size("gz"), lax.axis_size("gx")
    height = count_z // run
    y, h = lax.rem(k, run), lax.div(k, run)
    at_top = k == count_z - 1
    ph, so, p1, s1, fb = (r[n] for n in ("ph", "so", "p1", "s1", "fb"))
    lsem, osem = r["lsem"], r["osem"]

    own = slice(TOP, TOP + NR)
    load_phase = pltpu.make_async_copy(r["phase"], ph.at[2 : 2 + NP, own, :], lsem.at[0])
    load_solute = pltpu.make_async_copy(r["solute"], so.at[1 : 1 + NP, own, :], lsem.at[1])
    stage = [
        pltpu.make_async_copy(r["phase"].at[0:2], r["hsd"].at[0:2], lsem.at[6]),
        pltpu.make_async_copy(r["solute"].at[0:1], r["hsd"].at[2:3], lsem.at[7]),
        pltpu.make_async_copy(r["phase"].at[NP - 2 : NP], r["hsu"].at[0:2], lsem.at[8]),
        pltpu.make_async_copy(r["solute"].at[NP - 1 : NP], r["hsu"].at[2:3], lsem.at[9]),
    ]
    loads = [
        pltpu.make_async_copy(r[a], r[b], lsem.at[2 + n])
        for n, (a, b) in enumerate((("w1", "v1"), ("cs", "vcs"), ("back", "vback"), ("w2", "v2")))
    ]
    for copy in (load_phase, load_solute, *stage, *loads):
        copy.start()

    barrier = pltpu.get_barrier_semaphore()

    def greet_x(j, carry):
        other = lax.rem(i + j, count_x)
        pl.semaphore_signal(barrier, inc=1, device_id={"gx": other}, device_id_type=MESH)
        return carry

    lax.fori_loop(1, count_x, greet_x, 0)

    def greet_y(j, carry):
        other = h * run + lax.rem(y + j, run)
        pl.semaphore_signal(barrier, inc=1, device_id={"gz": other}, device_id_type=MESH)
        return carry

    lax.fori_loop(1, run, greet_y, 0)
    def is_column(up):
        return functools.reduce(jnp.logical_or, [y == (run - 1 - c if up else c) for c in seam_columns(run)])

    def greet(other):
        pl.semaphore_signal(barrier, inc=1, device_id={"gz": other}, device_id_type=MESH)

    greetings = (count_x - 1) + (run - 1)
    for up in (False, True):
        near, far = (h < height - 1, h > 0) if up else (h > 0, h < height - 1)
        step = 1 if up else -1
        last = 0 if up else run - 1

        @pl.when(jnp.logical_and(near, is_column(up)))
        def _(step=step, last=last):
            greet((h + step) * run + last)

        @pl.when(jnp.logical_and(far, y == last))
        def _(up=up, step=step):
            for c in seam_columns(run):
                greet((h - step) * run + (run - 1 - c if up else c))

        greetings = greetings + jnp.where(jnp.logical_and(near, is_column(up)), 1, 0)
        greetings = greetings + jnp.where(jnp.logical_and(far, y == last), 4, 0)

    load_phase.wait()
    load_solute.wait()
    for copy in stage:
        copy.wait()
    for p in range(NP):
        at = slice(p, p + 1)
        r["xsl"][0, at, :] = ph[p + 2, TOP : TOP + 1, :]
        r["xsl"][1, at, :] = ph[p + 2, TOP + 1 : TOP + 2, :]
        r["xsl"][2, at, :] = so[p + 1, TOP : TOP + 1, :]
        r["xsh"][0, at, :] = ph[p + 2, TOP + NR - 1 : TOP + NR, :]
        r["xsh"][1, at, :] = ph[p + 2, TOP + NR - 2 : TOP + NR - 1, :]
        r["xsh"][2, at, :] = so[p + 1, TOP + NR - 1 : TOP + NR, :]
    r["ixs"][...] = jnp.full(PIECE, r["plane"][0], jnp.int32)

    pl.semaphore_wait(barrier, greetings)

    env = {
        "msem": r["msem"],
        "ra": [r["ra%d" % n] for n in range(8)],
        "run": run,
        "height": height,
        "y": y,
        "h": h,
    }
    down = Message(env, 0, False, r["hsd"], r["hrd"])
    upward = Message(env, 1, True, r["hsu"], r["hru"])
    second = Message(env, 2, False, r["c2s"], r["c2r"])
    first = Message(env, 3, False, r["c1s"], r["c1r"])
    bulk = [
        Message(env, 4, False, fb.at[0:2], fb.at[8:10]),
        Message(env, 5, False, fb.at[2:6], fb.at[10:14]),
        Message(env, 6, False, fb.at[6:8], fb.at[14:16]),
    ]
    onward = Message(env, 7, False, fb.at[8:10], fb.at[16:18])

    def remote(src, dst, n, target):
        return pltpu.make_async_remote_copy(
            src_ref=src,
            dst_ref=dst,
            send_sem=osem.at[2 * n],
            recv_sem=osem.at[2 * n + 1],
            device_id=target,
            device_id_type=MESH,
        )

    above = {"gz": lax.rem(k + 1, count_z)}
    below = {"gz": lax.rem(k + count_z - 1, count_z)}
    not_top = jnp.logical_not(at_top)
    not_low = k > 0

    down.start_seam()
    upward.start_seam()
    before = {"gx": lax.rem(i + count_x - 1, count_x)}
    after = {"gx": lax.rem(i + 1, count_x)}
    to_before = remote(r["xsl"], r["xrh"], 0, before)
    to_after = remote(r["xsh"], r["xrl"], 1, after)
    to_before.start()
    to_after.start()
    index_first = remote(r["ixs"], r["ixa"], 2, above)
    index_second = remote(r["ixa"], r["ixb"], 3, above)

    @pl.when(not_top)
    def _():
        index_first.start()

    to_before.wait_recv()
    to_after.wait_recv()
    r["cse"][0:1, :] = r["xrl"][0, 0:1, :]
    r["cse"][1:2, :] = r["xrh"][0, 0:1, :]
    r["csu"][0:1, :] = r["xrl"][0, NP - 1 : NP, :]
    r["csu"][1:2, :] = r["xrh"][0, NP - 1 : NP, :]
    corner_down = remote(r["cse"], r["cre"], 4, below)
    corner_up = remote(r["csu"], r["cru"], 5, above)

    @pl.when(not_low)
    def _():
        corner_down.start()

    @pl.when(not_top)
    def _():
        corner_up.start()

    down.relay()
    upward.relay()
    down.start_inside()
    upward.start_inside()

    for p in range(NP):
        ph[p + 2, TOP - 1 : TOP, :] = r["xrl"][0, p : p + 1, :]
        ph[p + 2, TOP + NR : TOP + NR + 1, :] = r["xrh"][0, p : p + 1, :]

    @pl.when(not_low)
    def _():
        index_first.wait_recv()

    @pl.when(jnp.logical_and(not_top, not_low))
    def _():
        index_second.start()

    pull_first = r["pulls"][0]
    pull_both = pull_first + r["pulls"][1]

    def thermal_of(plane):
        return ((2 * plane - count_z * NP).astype(F32)) * (1.0 / (count_z * NP))

    def row_groups():
        return [TOP + 8 * g for g in range(NR // 8)]

    def first_step(p, with_solute):
        thermal = thermal_of(k * NP + p - pull_first)
        for a in row_groups():
            rows = slice(a, a + 8)
            centre = ph[p + 2, rows, :]
            sides = [
                ph[p + 1, rows, :],
                ph[p + 3, rows, :],
                ph[p + 2, a - 1 : a + 7, :],
                ph[p + 2, a + 1 : a + 9, :],
                *lane_sides(centre),
            ]
            here = so[p + 1, rows, :]
            total = sum(sides)
            driving = driving_of(centre, total, here, thermal)
            p1[p + 1, rows, :] = advance_phase(centre, driving)
            if with_solute:
                solute_sides = [
                    so[p, rows, :],
                    so[p + 2, rows, :],
                    so[p + 1, a - 1 : a + 7, :],
                    so[p + 1, a + 1 : a + 9, :],
                    *lane_sides(here),
                ]
                mixed = sum(u * v for u, v in zip(sides, solute_sides))
                spread = sum(solute_sides) - 6.0 * here
                flux = 0.25 * ((2.0 - centre) * spread - mixed + here * total)
                rate = (DIFFUSIVITY * flux + 0.5 * (1.0 + (1.0 - PARTITION) * here) * driving) / (
                    0.5 * (1.0 + PARTITION) - 0.5 * (1.0 - PARTITION) * centre
                )
                s1[p, a - TOP : a - TOP + 8, :] = here + TIME_STEP * rate

    def second_step(p):
        plane = k * NP + p
        thermal = thermal_of(plane - pull_both)
        for a in row_groups():
            rows = slice(a, a + 8)
            centre = p1[p + 1, rows, :]
            low = jnp.where(plane == pull_both, centre, p1[p, rows, :])
            total = sum(
                [
                    low,
                    p1[p + 2, rows, :],
                    p1[p + 1, a - 1 : a + 7, :],
                    p1[p + 1, a + 1 : a + 9, :],
                    *lane_sides(centre),
                ]
            )
            driving = driving_of(centre, total, s1[p, a - TOP : a - TOP + 8, :], thermal)
            fb[p, a - TOP : a - TOP + 8, :] = advance_phase(centre, driving)

    def second_body(p, carry):
        second_step(p)
        return carry

    for p in range(NP):
        so[p + 1, TOP - 1 : TOP, :] = r["xrl"][2, p : p + 1, :]
        so[p + 1, TOP + NR : TOP + NR + 1, :] = r["xrh"][2, p : p + 1, :]

    def first_body(p, carry):
        first_step(p, True)
        return carry

    plane_row = lax.broadcasted_iota(jnp.int32, (NP, NL), 0)
    thermal_rows = (2 * (plane_row + (k * NP - pull_first)) - count_z * NP).astype(F32) * (
        1.0 / (count_z * NP)
    )

    def rows_beside(planes, with_ends):
        for side, (got, sent, at) in enumerate(
            ((r["xrl"], r["xsl"], TOP - 1), (r["xrh"], r["xsh"], TOP + NR))
        ):
            centre = got[0]
            low, high = pltpu.roll(centre, 1, 0), pltpu.roll(centre, NP - 1, 0)
            if with_ends:
                low = jnp.where(plane_row == 0, r["cru"][side : side + 1, :], low)
                high = jnp.where(plane_row == NP - 1, r["cre"][side : side + 1, :], high)
            total = sum([low, high, got[1], sent[0], *lane_sides(centre)])
            driving = driving_of(centre, total, got[2], thermal_rows)
            moved = advance_phase(centre, driving)
            for p in planes:
                p1[p + 1, at : at + 1, :] = moved[p : p + 1, :]

    lax.fori_loop(1, NP - 1, first_body, 0)
    rows_beside(range(1, NP - 1), False)
    lax.fori_loop(2, NP - 2, second_body, 0)

    @pl.when(at_top)
    def _():
        ph[NP + 2 : NP + 4] = jnp.full((2, 2 * TOP + NR, NL), FAR, F32)
        so[NP + 1 : NP + 3] = jnp.full((2, 2 * TOP + NR, NL), FAR, F32)
        r["cre"][...] = jnp.full((2, NL), FAR, F32)
        p1[NP + 2 : NP + 4] = jnp.full((2, 2 * TOP + NR, NL), FAR, F32)
        s1[NP + 1 : NP + 2] = jnp.full((1, NR, NL), FAR, F32)

    @pl.when(k == 0)
    def _():
        ph[0:2] = jnp.full((2, 2 * TOP + NR, NL), FAR, F32)
        so[0:1] = jnp.full((1, 2 * TOP + NR, NL), FAR, F32)
        r["cru"][...] = jnp.full((2, NL), FAR, F32)

    @pl.when(not_low)
    def _():
        corner_up.wait_recv()

    @pl.when(not_top)
    def _():
        corner_down.wait_recv()

    down.arrive()
    upward.arrive()

    @pl.when(not_top)
    def _():
        ph[NP + 2, own, :] = r["hrd"][0]
        ph[NP + 3, own, :] = r["hrd"][1]
        so[NP + 1, own, :] = r["hrd"][2]

    @pl.when(not_low)
    def _():
        ph[0, own, :] = r["hru"][0]
        ph[1, own, :] = r["hru"][1]
        so[0, own, :] = r["hru"][2]

    ph[1, TOP - 1 : TOP, :] = r["cru"][0:1, :]
    ph[1, TOP + NR : TOP + NR + 1, :] = r["cru"][1:2, :]
    ph[NP + 2, TOP - 1 : TOP, :] = r["cre"][0:1, :]
    ph[NP + 2, TOP + NR : TOP + NR + 1, :] = r["cre"][1:2, :]

    first_step(-1, False)
    first_step(0, True)
    first_step(NP - 1, True)
    rows_beside((0, NP - 1), True)

    @pl.when(not_top)
    def _():
        first_step(NP, False)

    @pl.when(at_top)
    def _():
        first_step(NP, True)
        for got, at in ((r["xrl"], TOP - 1), (r["xrh"], TOP + NR)):
            centre = jnp.full((NP, NL), FAR, F32)
            low = jnp.where(plane_row == 0, pltpu.roll(got[0], 1, 0), FAR)
            total = low + 5.0 * FAR
            driving = driving_of(centre, total, centre, 0.0)
            p1[NP + 1, at : at + 1, :] = advance_phase(centre, driving)[0:1, :]

    lax.fori_loop(0, 2, second_body, 0)

    def mask_of(which, local):
        return jnp.broadcast_to(which[0:1, 0:1] == local, (NR, NL))

    @pl.when(k == 0)
    def _():
        r["ixa"][...] = jnp.zeros(PIECE, jnp.int32)

    @pl.when(k > 1)
    def _():
        index_second.wait_recv()

    @pl.when(k <= 1)
    def _():
        r["ixb"][...] = jnp.zeros(PIECE, jnp.int32)

    two = r["ixb"][...] + (pull_both - k * NP)
    one = r["ixa"][...] + (pull_both - k * NP)
    none = r["ixs"][...] + (pull_both - k * NP)
    r["c2s"][0] = jnp.where(mask_of(two, 1), fb[1], fb[0])
    second.start()
    second.relay()
    lax.fori_loop(NP - 2, NP, second_body, 0)

    @pl.when(at_top)
    def _():
        second_step(NP)
        second_step(NP + 1)
        fb[NP + 2 : NP + 10] = jnp.full((8, NR, NL), FAR, F32)
        r["c2r"][0] = jnp.where(mask_of(one, NP), fb[NP], fb[NP + 1])
        r["c1r"][0] = jnp.where(
            mask_of(none, NP), fb[NP], jnp.where(mask_of(none, NP + 1), fb[NP + 1], FAR)
        )

    picked = fb[0]
    for p in range(1, NP):
        picked = jnp.where(mask_of(one, p), fb[p], picked)
    r["c1s"][0] = picked
    first.relay((1,))
    for message in bulk:
        message.relay((1,))
    second.arrive()
    beyond = jnp.broadcast_to(one[0:1, 0:1] >= NP, (NR, NL))
    r["c1s"][0] = jnp.where(beyond, r["c2r"][0], r["c1s"][0])
    first.start()
    for message in bulk:
        message.start()
    first.relay((2, 3))
    first.arrive()
    inside = jnp.broadcast_to(none[0:1, 0:1] < NP, (NR, NL))
    section = jnp.where(
        inside, jnp.where(mask_of(none, NP - 1), fb[NP - 1], fb[NP - 2]), r["c1r"][0]
    )

    for load in loads:
        load.wait()

    def exchange(src, dst, n, start):
        def one_copy(j, carry):
            other = lax.rem(i + j, count_x)
            remote(src.at[other], dst.at[i], n, {"gx": other}).start()
            return carry

        if start:
            lax.fori_loop(1, count_x, one_copy, 0)
            dst[i] = src[i]
        else:
            some = slice(0, count_x - 1)
            remote(src.at[some], dst.at[some], n, before).wait_recv()

    row_sum = jnp.sum(section, axis=1, keepdims=True)
    level = section - row_sum * (1.0 / NL)
    near, far = level[:, :HALF], level[:, HALF:]
    spectrum = jnp.concatenate([mm(near + far, r["v1"], 0), mm(near - far, r["v1"], 1)], 1)
    lane = lax.broadcasted_iota(jnp.int32, (NR, NL), 1)
    spectrum = jnp.where(lane == 0, row_sum, spectrum)
    if with_corr:
        pack(spectrum, r["sd1"])
        exchange(r["sd1"], r["rv1"], 6, True)
    for message in bulk:
        message.relay((2, 3))
    if with_corr:
        exchange(r["sd1"], r["rv1"], 6, False)

        rows = unpack(r["rv1"])
        row = lax.broadcasted_iota(jnp.int32, (NR, NL), 0)
        lowest = jnp.logical_and(row == 0, jnp.broadcast_to(i, (NR, NL)) == 0)
        mean = jnp.sum(rows, axis=1, keepdims=True) * (1.0 / NL)
        rows = jnp.where(lowest, rows - mean, rows)
        starts = [256 * g for g in range(4)]
        near = jnp.concatenate([rows[:, s : s + 128] for s in starts], 1)
        far = jnp.concatenate([rows[:, s + 128 : s + 256] for s in starts], 1)
        special_row = jnp.logical_and(
            lax.broadcasted_iota(jnp.int32, (16, HALF), 0) == 0,
            jnp.broadcast_to(i, (16, HALF)) == 0,
        )
        first_lane = lax.broadcasted_iota(jnp.int32, (16, HALF), 1) == 0
        halves = []
        for odd, part in enumerate((near + far, near - far)):
            z = mm(part, r["vcs"], odd)
            ac, as_ = z[:16, :HALF], z[:16, HALF:]
            bc, bs = z[16:, :HALF], z[16:, HALF:]
            real, imag = ac + bs, bc - as_
            power = real * real + imag * imag
            lone = ac * ac + as_ * as_
            if not odd:
                lone = jnp.where(first_lane, 0.0, lone)
            power = jnp.where(special_row, lone, power)
            halves.append(mm(jnp.concatenate([power, bc * bc + bs * bs], 0), r["vback"], odd))
        even, odd_part = halves
        lags = jnp.concatenate(
            [
                even[:, :HALF] + odd_part[:, :HALF],
                even[:, :HALF] - odd_part[:, :HALF],
            ],
            1,
        )
        sines = jnp.concatenate(
            [
                even[:16, HALF:] + odd_part[:16, HALF:],
                even[:16, HALF:] - odd_part[:16, HALF:],
            ],
            1,
        )
        special_wide = jnp.logical_and(
            lax.broadcasted_iota(jnp.int32, (16, NL), 0) == 0,
            jnp.broadcast_to(i, (16, NL)) == 0,
        )
        sines = jnp.where(special_wide, lags[16:], sines)
        pack(jnp.concatenate([lags[:16], sines], 0), r["sd2"])
        exchange(r["sd2"], r["rv2"], 7, True)
    bulk[0].arrive()
    onward.start()
    if with_corr:
        exchange(r["sd2"], r["rv2"], 7, False)
        rows = unpack(r["rv2"])
        even = jnp.concatenate([rows[:, s : s + 128] for s in starts], 1)
        odd_part = jnp.concatenate([rows[:, s + 128 : s + 256] for s in starts], 1)
        even = mm(even, r["v2"], 0)
        odd_part = mm(odd_part, r["v2"], 1)
        r["corr"][0, :, :HALF] = even + odd_part
        r["corr"][0, :, HALF:] = even - odd_part
    else:
        r["corr"][0] = section
    onward.relay()
    bulk[1].arrive()
    bulk[2].arrive()
    onward.arrive()
    r["final"][...] = fb[pl.ds(pull_both, NP)]

    for message in (down, upward, second, first, *bulk, onward):
        message.finish()
    to_before.wait_send()
    to_after.wait_send()

    @pl.when(not_top)
    def _():
        index_first.wait_send()
        corner_up.wait_send()

    @pl.when(jnp.logical_and(not_top, not_low))
    def _():
        index_second.wait_send()

    @pl.when(not_low)
    def _():
        corner_down.wait_send()

    if with_corr:
        for n, src in ((6, r["sd1"]), (7, r["sd2"])):
            some = src.at[0 : count_x - 1]
            remote(some, some, n, before).wait_send()


def per_device(run, with_corr, phase_field, solute, pull_counts, planes):
    w1, cs, back, w2 = (jnp.asarray(t) for t in tables())
    wide = 2 * TOP + NR
    vmem = lambda *shape: pltpu.VMEM(shape, F32)
    scratch = [
        vmem(NP + 4, wide, NL),
        vmem(NP + 3, wide, NL),
        vmem(NP + 4, wide, NL),
        vmem(NP + 2, NR, NL),
        vmem(18, NR, NL),
        *[vmem(3, NR, NL) for _ in range(4)],
        *[vmem(3, NP, NL) for _ in range(4)],
        *[vmem(2, NL) for _ in range(4)],
        *[pltpu.VMEM(PIECE, jnp.int32) for _ in range(3)],
        *[vmem(1, NR, NL) for _ in range(4)],
        *[vmem(32, *PIECE) for _ in range(4)],
        *[pltpu.VMEM(t.shape, BF16) for t in (w1, cs, back, w2)],
        *[vmem(n, 8, NL) for n in MESSAGES],
        pltpu.SemaphoreType.DMA((8, 4)),
        pltpu.SemaphoreType.DMA((16,)),
        pltpu.SemaphoreType.DMA((10,)),
    ]
    smem = pl.BlockSpec(memory_space=pltpu.SMEM)
    anywhere = pl.BlockSpec(memory_space=pl.ANY)
    local = pl.BlockSpec(memory_space=pltpu.VMEM)
    return pl.pallas_call(
        functools.partial(kernel, run, with_corr),
        out_shape=(
            jax.ShapeDtypeStruct((NP, NR, NL), F32),
            jax.ShapeDtypeStruct((1, NR, NL), F32),
        ),
        in_specs=[smem, smem, *[anywhere] * 6],
        out_specs=(local, local),
        scratch_shapes=scratch,
        compiler_params=pltpu.CompilerParams(
            collective_id=0, has_side_effects=True, vmem_limit_bytes=56 * 1024 * 1024
        ),
    )(pull_counts, planes, phase_field, solute, w1, cs, back, w2)


def build(mesh, run, with_corr):
    return jax.shard_map(
        functools.partial(per_device, run, with_corr),
        mesh=mesh,
        in_specs=(P("gz", "gx", None), P("gz", "gx", None), P(), P("gz")),
        out_specs=(P("gz", "gx", None), P("gz", "gx", None)),
        check_vma=False,
    )


def solution(mesh):
    return build(mesh, RUN, True)
```

```python
import functools
import math

import jax
import jax.numpy as jnp
import ml_dtypes
import numpy as np
from jax import lax
from jax.experimental import pallas as pl
from jax.experimental.pallas import tpu as pltpu
from jax.sharding import PartitionSpec as P

MESH = pl.DeviceIdType.MESH
F32 = jnp.float32
BF16 = jnp.bfloat16

TIME_STEP = 0.05
PARTITION = 0.15
COUPLING = 1.6
DIFFUSIVITY = 0.4
FAR = -1.0

NP, NR, NL = 8, 32, 1024
HALF = NL // 2
RUN = 8
TOP = 8
PIECE = (8, 128)


def split_bf16(table):
    high = table.astype(ml_dtypes.bfloat16)
    low = (table - high.astype(np.float64)).astype(ml_dtypes.bfloat16)
    return np.stack([high, low])


@functools.lru_cache(None)
def tables():
    w = 2.0 * math.pi / NL
    parts, part_rows = 16, 32
    m = np.arange(parts)[:, None]
    l = np.arange(part_rows)[None, :]
    order = np.arange(HALF)
    near = np.arange(HALF)

    def trig(a, b):
        angle = (a[:, None] * b[None, :]) % NL
        return np.cos(w * angle), np.sin(w * angle)

    w1, w2 = [], []
    for odd in (0, 1):
        ky = np.broadcast_to(2 * (16 * m + l % 16) + odd, (parts, part_rows)).reshape(-1)
        imag = np.broadcast_to(l >= 16, (parts, part_rows)).reshape(-1)
        c, s = trig(near, ky)
        fwd = np.where(imag[None, :], -s, c)
        inv = 2.0 * np.where(imag[None, :], -s, c)
        if not odd:
            fwd[:, 16] = (-1.0) ** near
            inv[:, 0] = 1.0
            inv[:, 16] = (-1.0) ** near
        w1.append(fwd)
        inv = inv.reshape(HALF, parts, 4, 8).transpose(0, 2, 1, 3).reshape(HALF, HALF)
        w2.append(inv.T / (NL * NL * float(NL)))
    g, i, r = np.meshgrid(np.arange(4), np.arange(parts), np.arange(8), indexing="ij")
    x = (32 * i + 8 * g + r).reshape(-1)
    cs, back = [], []
    for odd in (0, 1):
        kx = 2 * order + odd
        cs.append(np.concatenate(trig(x, kx), 1))
        back.append(np.concatenate(trig(kx, near), 1))
    return tuple(split_bf16(np.stack(t)) for t in (w1, cs, back, w2))


def mm(x, table, odd):
    rows = x.shape[0]
    high = x.astype(BF16)
    low = (x - high.astype(F32)).astype(BF16)
    both = jnp.concatenate([high, low], 0)
    first = jnp.dot(both, table[0, odd], preferred_element_type=F32)
    second = jnp.dot(high, table[1, odd], preferred_element_type=F32)
    return first[:rows] + first[rows:] + second


def pack(block, out, base=0):
    lane_group = lax.broadcasted_iota(jnp.int32, PIECE, 1) // 32
    for c in range(block.shape[1] // 128):
        v = [block[8 * g : 8 * g + 8, 128 * c : 128 * c + 128] for g in range(4)]
        for b in range(4):
            tile = v[b]
            for g in range(4):
                if g != b:
                    moved = pltpu.roll(v[g], (32 * (g - b)) % 128, 1)
                    tile = jnp.where(lane_group == g, moved, tile)
            out[base + 4 * c + b] = tile


def unpack(tiles):
    flat = tiles[...].reshape(256, 128)
    turned = flat.T
    return jnp.concatenate([turned[32 * g : 32 * g + 32] for g in range(4)], 1)


def seam_columns(run, kind):
    if run < 8 or kind == "small":
        return (0, run - 1, run // 2 - 1, run // 2)
    if kind == "onward":
        return (0, 2, 3, 4)
    return (0, 7, 3, 4, 2, 5, 1, 6)


def greeting_columns(run, up):
    kinds = ("small",) if up else ("small", "onward", "bulk")
    return tuple(sorted({c for kind in kinds for c in seam_columns(run, kind)}))


class Message:
    def __init__(self, env, index, up, src, dst, kind):
        self.src, self.dst, self.up = src, dst, up
        self.sems = [env["msem"].at[index, j] for j in range(4)]
        self.relay_ref = env["ra"][index]
        self.run, self.height = env["run"], env["height"]
        self.y = (self.run - 1 - env["y"]) if up else env["y"]
        self.h = (self.height - 1 - env["h"]) if up else env["h"]
        self.columns = seam_columns(self.run, kind)
        self.width = NL * 4 // len(self.columns)

    def copy(self, src, dst, send, recv, y, h):
        if self.up:
            y, h = self.run - 1 - y, self.height - 1 - h
        return pltpu.make_async_remote_copy(
            src_ref=src,
            dst_ref=dst,
            send_sem=self.sems[send],
            recv_sem=self.sems[recv],
            device_id={"gz": h * self.run + y},
            device_id_type=MESH,
        )

    def piece(self, ref, n):
        g, part = n % 4, n // 4
        return ref.at[:, 8 * g : 8 * g + 8, self.width * part : self.width * (part + 1)]

    def relayed(self, early=None):
        pieces = range(1, len(self.columns))
        if early is None:
            return list(pieces)
        return [n for n in pieces if (self.columns[n] == self.run - 1) == early]

    def has_target(self):
        return jnp.logical_or(self.y > 0, self.h > 0)

    def has_source(self):
        return jnp.logical_or(self.y < self.run - 1, self.h < self.height - 1)

    def start(self):
        self.start_seam(True)
        self.start_seam(False)
        self.start_inside()

    def start_inside(self):
        @pl.when(self.y > 0)
        def _():
            self.copy(self.src, self.dst, 0, 1, self.y - 1, self.h).start()

    def start_seam(self, early):
        @pl.when(jnp.logical_and(self.y == 0, self.h > 0))
        def _():
            for n in self.relayed(early):
                column = self.columns[n]
                self.copy(self.piece(self.src, n), self.relay_ref, 0, 3, column, self.h).start()
            if not early:
                there = self.piece(self.dst, 0)
                end = self.run - 1
                self.copy(self.piece(self.src, 0), there, 0, 1, end, self.h - 1).start()

    def relay(self, early=None):
        end = self.run - 1
        for n in self.relayed(early):

            @pl.when(jnp.logical_and(self.h > 0, self.y == self.columns[n]))
            def _(n=n):
                self.copy(self.relay_ref, self.relay_ref, 2, 3, end, self.h - 1).wait_recv()
                there = self.piece(self.dst, n)
                self.copy(self.relay_ref, there, 2, 1, end, self.h - 1).start()

    def arrive(self):
        @pl.when(self.has_source())
        def _():
            self.copy(self.src, self.dst, 0, 1, 0, 0).wait_recv()

    def finish(self):
        @pl.when(self.has_target())
        def _():
            self.copy(self.src, self.dst, 0, 1, 0, 0).wait_send()

        column = [self.y == self.columns[n] for n in self.relayed()]

        @pl.when(jnp.logical_and(self.h > 0, functools.reduce(jnp.logical_or, column)))
        def _():
            self.copy(self.relay_ref, self.relay_ref, 2, 3, 0, 0).wait_send()


MESSAGES = (3, 3, 1, 1, 2, 4, 2, 2)


def lane_sides(v):
    return pltpu.roll(v, 1, 1), pltpu.roll(v, NL - 1, 1)


def driving_of(centre, total, solute_now, thermal):
    gap = 1.0 - centre * centre
    return (total - 6.0 * centre) + centre * gap - COUPLING * (gap * gap) * (solute_now + thermal)


def advance_phase(centre, driving):
    return jnp.clip(centre + TIME_STEP * driving, -1.0, 1.0)


NAMES = (
    "pulls", "plane", "phase", "solute", "w1", "cs", "back", "w2", "final", "corr", "ph", "so",
    "p1", "s1", "fb", "hsd", "hsu", "hrd", "hru", "xsl", "xsh", "xrl", "xrh", "cse", "csu",
    "cre", "cru", "ixs", "ixa", "ixb", "c2s", "c2r", "c1s", "c1r", "sd1", "rv1", "sd2", "rv2",
    "v1", "vcs", "vback", "v2",
    *["ra%d" % n for n in range(8)],
    "msem", "osem", "lsem",
)


def kernel(run, with_corr, *refs):
    r = dict(zip(NAMES, refs, strict=True))
    k = lax.axis_index("gz")
    i = lax.axis_index("gx")
    count_z, count_x = lax.axis_size("gz"), lax.axis_size("gx")
    height = count_z // run
    y, h = lax.rem(k, run), lax.div(k, run)
    at_top = k == count_z - 1
    ph, so, p1, s1, fb = (r[n] for n in ("ph", "so", "p1", "s1", "fb"))
    lsem, osem = r["lsem"], r["osem"]

    own = slice(TOP, TOP + NR)
    load_phase = pltpu.make_async_copy(r["phase"], ph.at[2 : 2 + NP, own, :], lsem.at[0])
    load_solute = pltpu.make_async_copy(r["solute"], so.at[1 : 1 + NP, own, :], lsem.at[1])
    stage = [
        pltpu.make_async_copy(r["phase"].at[0:2], r["hsd"].at[0:2], lsem.at[6]),
        pltpu.make_async_copy(r["solute"].at[0:1], r["hsd"].at[2:3], lsem.at[7]),
        pltpu.make_async_copy(r["phase"].at[NP - 2 : NP], r["hsu"].at[0:2], lsem.at[8]),
        pltpu.make_async_copy(r["solute"].at[NP - 1 : NP], r["hsu"].at[2:3], lsem.at[9]),
    ]
    loads = [
        pltpu.make_async_copy(r[a], r[b], lsem.at[2 + n])
        for n, (a, b) in enumerate((("w1", "v1"), ("cs", "vcs"), ("back", "vback"), ("w2", "v2")))
    ]
    for copy in (load_phase, load_solute, *stage, *loads):
        copy.start()

    barrier = pltpu.get_barrier_semaphore()

    def is_column(up):
        return functools.reduce(jnp.logical_or, [y == (run - 1 - c if up else c) for c in greeting_columns(run, up)])

    def greet(other):
        pl.semaphore_signal(barrier, inc=1, device_id={"gz": other}, device_id_type=MESH)

    greetings = (count_x - 1) + (run - 1)
    for up in (False, True):
        near, far = (h < height - 1, h > 0) if up else (h > 0, h < height - 1)
        step = 1 if up else -1
        last = 0 if up else run - 1

        @pl.when(jnp.logical_and(near, is_column(up)))
        def _(step=step, last=last):
            greet((h + step) * run + last)

        @pl.when(jnp.logical_and(far, y == last))
        def _(up=up, step=step):
            for c in greeting_columns(run, up):
                greet((h - step) * run + (run - 1 - c if up else c))

        greetings = greetings + jnp.where(jnp.logical_and(near, is_column(up)), 1, 0)
        greetings = greetings + jnp.where(jnp.logical_and(far, y == last), len(greeting_columns(run, up)), 0)

    def greet_y(j, carry):
        other = h * run + lax.rem(y + j, run)
        pl.semaphore_signal(barrier, inc=1, device_id={"gz": other}, device_id_type=MESH)
        return carry

    lax.fori_loop(1, run, greet_y, 0)
    def greet_x(j, carry):
        other = lax.rem(i + j, count_x)
        pl.semaphore_signal(barrier, inc=1, device_id={"gx": other}, device_id_type=MESH)
        return carry

    lax.fori_loop(1, count_x, greet_x, 0)

    load_phase.wait()
    load_solute.wait()
    for copy in stage:
        copy.wait()
    for p in range(NP):
        at = slice(p, p + 1)
        r["xsl"][0, at, :] = ph[p + 2, TOP : TOP + 1, :]
        r["xsl"][1, at, :] = ph[p + 2, TOP + 1 : TOP + 2, :]
        r["xsl"][2, at, :] = so[p + 1, TOP : TOP + 1, :]
        r["xsh"][0, at, :] = ph[p + 2, TOP + NR - 1 : TOP + NR, :]
        r["xsh"][1, at, :] = ph[p + 2, TOP + NR - 2 : TOP + NR - 1, :]
        r["xsh"][2, at, :] = so[p + 1, TOP + NR - 1 : TOP + NR, :]
    r["ixs"][...] = jnp.full(PIECE, r["plane"][0], jnp.int32)

    pl.semaphore_wait(barrier, greetings)

    env = {
        "msem": r["msem"],
        "ra": [r["ra%d" % n] for n in range(8)],
        "run": run,
        "height": height,
        "y": y,
        "h": h,
    }
    down = Message(env, 0, False, r["hsd"], r["hrd"], "small")
    upward = Message(env, 1, True, r["hsu"], r["hru"], "small")
    second = Message(env, 2, False, r["c2s"], r["c2r"], "small")
    first = Message(env, 3, False, r["c1s"], r["c1r"], "small")
    bulk = [
        Message(env, 4, False, fb.at[0:2], fb.at[8:10], "bulk"),
        Message(env, 5, False, fb.at[2:6], fb.at[10:14], "bulk"),
        Message(env, 6, False, fb.at[6:8], fb.at[14:16], "bulk"),
    ]
    onward = Message(env, 7, False, fb.at[8:10], fb.at[16:18], "onward")

    def remote(src, dst, n, target):
        return pltpu.make_async_remote_copy(
            src_ref=src,
            dst_ref=dst,
            send_sem=osem.at[2 * n],
            recv_sem=osem.at[2 * n + 1],
            device_id=target,
            device_id_type=MESH,
        )

    above = {"gz": lax.rem(k + 1, count_z)}
    below = {"gz": lax.rem(k + count_z - 1, count_z)}
    not_top = jnp.logical_not(at_top)
    not_low = k > 0

    for message in (down, upward):
        message.start_seam(False)
        message.start_seam(True)
    before = {"gx": lax.rem(i + count_x - 1, count_x)}
    after = {"gx": lax.rem(i + 1, count_x)}
    to_before = remote(r["xsl"], r["xrh"], 0, before)
    to_after = remote(r["xsh"], r["xrl"], 1, after)
    to_before.start()
    to_after.start()
    index_first = remote(r["ixs"], r["ixa"], 2, above)
    index_second = remote(r["ixa"], r["ixb"], 3, above)

    @pl.when(not_top)
    def _():
        index_first.start()

    to_before.wait_recv()
    to_after.wait_recv()
    r["cse"][0:1, :] = r["xrl"][0, 0:1, :]
    r["cse"][1:2, :] = r["xrh"][0, 0:1, :]
    r["csu"][0:1, :] = r["xrl"][0, NP - 1 : NP, :]
    r["csu"][1:2, :] = r["xrh"][0, NP - 1 : NP, :]
    corner_down = remote(r["cse"], r["cre"], 4, below)
    corner_up = remote(r["csu"], r["cru"], 5, above)

    @pl.when(not_low)
    def _():
        corner_down.start()

    @pl.when(not_top)
    def _():
        corner_up.start()

    down.relay()
    upward.relay()
    down.start_inside()
    upward.start_inside()

    for p in range(NP):
        ph[p + 2, TOP - 1 : TOP, :] = r["xrl"][0, p : p + 1, :]
        ph[p + 2, TOP + NR : TOP + NR + 1, :] = r["xrh"][0, p : p + 1, :]

    @pl.when(not_low)
    def _():
        index_first.wait_recv()

    @pl.when(jnp.logical_and(not_top, not_low))
    def _():
        index_second.start()

    pull_first = r["pulls"][0]
    pull_both = pull_first + r["pulls"][1]

    def thermal_of(plane):
        return ((2 * plane - count_z * NP).astype(F32)) * (1.0 / (count_z * NP))

    def row_groups():
        return [TOP + 8 * g for g in range(NR // 8)]

    def first_step(p, with_solute):
        thermal = thermal_of(k * NP + p - pull_first)
        for a in row_groups():
            rows = slice(a, a + 8)
            centre = ph[p + 2, rows, :]
            sides = [
                ph[p + 1, rows, :],
                ph[p + 3, rows, :],
                ph[p + 2, a - 1 : a + 7, :],
                ph[p + 2, a + 1 : a + 9, :],
                *lane_sides(centre),
            ]
            here = so[p + 1, rows, :]
            total = sum(sides)
            driving = driving_of(centre, total, here, thermal)
            p1[p + 1, rows, :] = advance_phase(centre, driving)
            if with_solute:
                solute_sides = [
                    so[p, rows, :],
                    so[p + 2, rows, :],
                    so[p + 1, a - 1 : a + 7, :],
                    so[p + 1, a + 1 : a + 9, :],
                    *lane_sides(here),
                ]
                mixed = sum(u * v for u, v in zip(sides, solute_sides))
                spread = sum(solute_sides) - 6.0 * here
                flux = 0.25 * ((2.0 - centre) * spread - mixed + here * total)
                rate = (DIFFUSIVITY * flux + 0.5 * (1.0 + (1.0 - PARTITION) * here) * driving) / (
                    0.5 * (1.0 + PARTITION) - 0.5 * (1.0 - PARTITION) * centre
                )
                s1[p, a - TOP : a - TOP + 8, :] = here + TIME_STEP * rate

    def second_step(p):
        plane = k * NP + p
        thermal = thermal_of(plane - pull_both)
        for a in row_groups():
            rows = slice(a, a + 8)
            centre = p1[p + 1, rows, :]
            low = jnp.where(plane == pull_both, centre, p1[p, rows, :])
            total = sum(
                [
                    low,
                    p1[p + 2, rows, :],
                    p1[p + 1, a - 1 : a + 7, :],
                    p1[p + 1, a + 1 : a + 9, :],
                    *lane_sides(centre),
                ]
            )
            driving = driving_of(centre, total, s1[p, a - TOP : a - TOP + 8, :], thermal)
            fb[p, a - TOP : a - TOP + 8, :] = advance_phase(centre, driving)

    def second_body(p, carry):
        second_step(p)
        return carry

    for p in range(NP):
        so[p + 1, TOP - 1 : TOP, :] = r["xrl"][2, p : p + 1, :]
        so[p + 1, TOP + NR : TOP + NR + 1, :] = r["xrh"][2, p : p + 1, :]

    def first_body(p, carry):
        first_step(p, True)
        return carry

    plane_row = lax.broadcasted_iota(jnp.int32, (NP, NL), 0)
    thermal_rows = (2 * (plane_row + (k * NP - pull_first)) - count_z * NP).astype(F32) * (
        1.0 / (count_z * NP)
    )

    def rows_beside(planes, with_ends):
        for side, (got, sent, at) in enumerate(
            ((r["xrl"], r["xsl"], TOP - 1), (r["xrh"], r["xsh"], TOP + NR))
        ):
            centre = got[0]
            low, high = pltpu.roll(centre, 1, 0), pltpu.roll(centre, NP - 1, 0)
            if with_ends:
                low = jnp.where(plane_row == 0, r["cru"][side : side + 1, :], low)
                high = jnp.where(plane_row == NP - 1, r["cre"][side : side + 1, :], high)
            total = sum([low, high, got[1], sent[0], *lane_sides(centre)])
            driving = driving_of(centre, total, got[2], thermal_rows)
            moved = advance_phase(centre, driving)
            for p in planes:
                p1[p + 1, at : at + 1, :] = moved[p : p + 1, :]

    lax.fori_loop(1, NP - 1, first_body, 0)
    rows_beside(range(1, NP - 1), False)
    lax.fori_loop(2, NP - 2, second_body, 0)

    @pl.when(at_top)
    def _():
        ph[NP + 2 : NP + 4] = jnp.full((2, 2 * TOP + NR, NL), FAR, F32)
        so[NP + 1 : NP + 3] = jnp.full((2, 2 * TOP + NR, NL), FAR, F32)
        r["cre"][...] = jnp.full((2, NL), FAR, F32)
        p1[NP + 2 : NP + 4] = jnp.full((2, 2 * TOP + NR, NL), FAR, F32)
        s1[NP + 1 : NP + 2] = jnp.full((1, NR, NL), FAR, F32)

    @pl.when(k == 0)
    def _():
        ph[0:2] = jnp.full((2, 2 * TOP + NR, NL), FAR, F32)
        so[0:1] = jnp.full((1, 2 * TOP + NR, NL), FAR, F32)
        r["cru"][...] = jnp.full((2, NL), FAR, F32)

    @pl.when(not_low)
    def _():
        corner_up.wait_recv()

    @pl.when(not_top)
    def _():
        corner_down.wait_recv()

    down.arrive()
    upward.arrive()

    @pl.when(not_top)
    def _():
        ph[NP + 2, own, :] = r["hrd"][0]
        ph[NP + 3, own, :] = r["hrd"][1]
        so[NP + 1, own, :] = r["hrd"][2]

    @pl.when(not_low)
    def _():
        ph[0, own, :] = r["hru"][0]
        ph[1, own, :] = r["hru"][1]
        so[0, own, :] = r["hru"][2]

    ph[1, TOP - 1 : TOP, :] = r["cru"][0:1, :]
    ph[1, TOP + NR : TOP + NR + 1, :] = r["cru"][1:2, :]
    ph[NP + 2, TOP - 1 : TOP, :] = r["cre"][0:1, :]
    ph[NP + 2, TOP + NR : TOP + NR + 1, :] = r["cre"][1:2, :]

    first_step(-1, False)
    first_step(0, True)
    first_step(NP - 1, True)
    rows_beside((0, NP - 1), True)

    @pl.when(not_top)
    def _():
        first_step(NP, False)

    @pl.when(at_top)
    def _():
        first_step(NP, True)
        for got, at in ((r["xrl"], TOP - 1), (r["xrh"], TOP + NR)):
            centre = jnp.full((NP, NL), FAR, F32)
            low = jnp.where(plane_row == 0, pltpu.roll(got[0], 1, 0), FAR)
            total = low + 5.0 * FAR
            driving = driving_of(centre, total, centre, 0.0)
            p1[NP + 1, at : at + 1, :] = advance_phase(centre, driving)[0:1, :]

    lax.fori_loop(0, 2, second_body, 0)

    def mask_of(which, local):
        return jnp.broadcast_to(which[0:1, 0:1] == local, (NR, NL))

    @pl.when(k == 0)
    def _():
        r["ixa"][...] = jnp.zeros(PIECE, jnp.int32)

    @pl.when(k > 1)
    def _():
        index_second.wait_recv()

    @pl.when(k <= 1)
    def _():
        r["ixb"][...] = jnp.zeros(PIECE, jnp.int32)

    two = r["ixb"][...] + (pull_both - k * NP)
    one = r["ixa"][...] + (pull_both - k * NP)
    none = r["ixs"][...] + (pull_both - k * NP)
    r["c2s"][0] = jnp.where(mask_of(two, 1), fb[1], fb[0])
    second.start()
    second.relay()
    lax.fori_loop(NP - 2, NP, second_body, 0)

    @pl.when(at_top)
    def _():
        second_step(NP)
        second_step(NP + 1)
        fb[NP + 2 : NP + 10] = jnp.full((8, NR, NL), FAR, F32)
        r["c2r"][0] = jnp.where(mask_of(one, NP), fb[NP], fb[NP + 1])
        r["c1r"][0] = jnp.where(
            mask_of(none, NP), fb[NP], jnp.where(mask_of(none, NP + 1), fb[NP + 1], FAR)
        )

    picked = fb[0]
    for p in range(1, NP):
        picked = jnp.where(mask_of(one, p), fb[p], picked)
    r["c1s"][0] = picked
    first.relay(True)
    for message in bulk:
        message.relay(True)
    second.arrive()
    beyond = jnp.broadcast_to(one[0:1, 0:1] >= NP, (NR, NL))
    r["c1s"][0] = jnp.where(beyond, r["c2r"][0], r["c1s"][0])
    first.start()
    for message in bulk:
        message.start_seam(True)
    for message in bulk:
        message.start_seam(False)
        message.start_inside()
    first.relay(False)
    first.arrive()
    inside = jnp.broadcast_to(none[0:1, 0:1] < NP, (NR, NL))
    section = jnp.where(
        inside, jnp.where(mask_of(none, NP - 1), fb[NP - 1], fb[NP - 2]), r["c1r"][0]
    )

    for load in loads:
        load.wait()

    def send_tiles(src, dst, n, first, count):
        def one_copy(j, carry):
            other = first + lax.rem(i + j, count)

            @pl.when(other != i)
            def _():
                remote(src.at[other], dst.at[i], n, {"gx": other}).start()

            return carry

        lax.fori_loop(1, count + 1, one_copy, 0)

    def await_tiles(src, dst, n):
        dst[i] = src[i]
        some = slice(0, count_x - 1)
        remote(src.at[some], dst.at[some], n, before).wait_recv()

    row_sum = jnp.sum(section, axis=1, keepdims=True)
    level = section - row_sum * (1.0 / NL)
    near, far = level[:, :HALF], level[:, HALF:]
    half = max(count_x // 2, 1)
    even = mm(near + far, r["v1"], 0)
    lane = lax.broadcasted_iota(jnp.int32, (NR, HALF), 1)
    pack(jnp.where(lane == 0, row_sum, even), r["sd1"])
    if with_corr:
        send_tiles(r["sd1"], r["rv1"], 6, 0, half)
    pack(mm(near - far, r["v1"], 1), r["sd1"], half)
    if with_corr:
        send_tiles(r["sd1"], r["rv1"], 6, half, half)
    for message in bulk:
        message.relay(False)

    @pl.when(y < run - 1)
    def _():
        bulk[0].arrive()

    onward.start_seam(True)
    onward.start_seam(False)

    @pl.when(y < run - 1)
    def _():
        onward.start_inside()

    if with_corr:
        await_tiles(r["sd1"], r["rv1"], 6)

        rows = unpack(r["rv1"])
        row = lax.broadcasted_iota(jnp.int32, (NR, NL), 0)
        lowest = jnp.logical_and(row == 0, jnp.broadcast_to(i, (NR, NL)) == 0)
        mean = jnp.sum(rows, axis=1, keepdims=True) * (1.0 / NL)
        rows = jnp.where(lowest, rows - mean, rows)
        starts = [256 * g for g in range(4)]
        near = jnp.concatenate([rows[:, s : s + 128] for s in starts], 1)
        far = jnp.concatenate([rows[:, s + 128 : s + 256] for s in starts], 1)
        special_row = jnp.logical_and(
            lax.broadcasted_iota(jnp.int32, (16, HALF), 0) == 0,
            jnp.broadcast_to(i, (16, HALF)) == 0,
        )
        first_lane = lax.broadcasted_iota(jnp.int32, (16, HALF), 1) == 0
        halves = []
        for odd, part in enumerate((near + far, near - far)):
            z = mm(part, r["vcs"], odd)
            ac, as_ = z[:16, :HALF], z[:16, HALF:]
            bc, bs = z[16:, :HALF], z[16:, HALF:]
            real, imag = ac + bs, bc - as_
            power = real * real + imag * imag
            lone = ac * ac + as_ * as_
            if not odd:
                lone = jnp.where(first_lane, 0.0, lone)
            power = jnp.where(special_row, lone, power)
            halves.append(mm(jnp.concatenate([power, bc * bc + bs * bs], 0), r["vback"], odd))
        even, odd_part = halves
        lags = jnp.concatenate(
            [
                even[:, :HALF] + odd_part[:, :HALF],
                even[:, :HALF] - odd_part[:, :HALF],
            ],
            1,
        )
        sines = jnp.concatenate(
            [
                even[:16, HALF:] + odd_part[:16, HALF:],
                even[:16, HALF:] - odd_part[:16, HALF:],
            ],
            1,
        )
        special_wide = jnp.logical_and(
            lax.broadcasted_iota(jnp.int32, (16, NL), 0) == 0,
            jnp.broadcast_to(i, (16, NL)) == 0,
        )
        sines = jnp.where(special_wide, lags[16:], sines)
        pack(jnp.concatenate([lags[:16], sines], 0), r["sd2"])
        send_tiles(r["sd2"], r["rv2"], 7, 0, count_x)
    onward.relay()

    @pl.when(y == run - 1)
    def _():
        bulk[0].arrive()
        onward.start_inside()

    if with_corr:
        await_tiles(r["sd2"], r["rv2"], 7)
        rows = unpack(r["rv2"])
        even = jnp.concatenate([rows[:, s : s + 128] for s in starts], 1)
        odd_part = jnp.concatenate([rows[:, s + 128 : s + 256] for s in starts], 1)
        even = mm(even, r["v2"], 0)
        odd_part = mm(odd_part, r["v2"], 1)
        r["corr"][0, :, :HALF] = even + odd_part
        r["corr"][0, :, HALF:] = even - odd_part
    else:
        r["corr"][0] = section
    bulk[1].arrive()
    bulk[2].arrive()
    onward.arrive()
    r["final"][...] = fb[pl.ds(pull_both, NP)]

    for message in (down, upward, second, first, *bulk, onward):
        message.finish()
    to_before.wait_send()
    to_after.wait_send()

    @pl.when(not_top)
    def _():
        index_first.wait_send()
        corner_up.wait_send()

    @pl.when(jnp.logical_and(not_top, not_low))
    def _():
        index_second.wait_send()

    @pl.when(not_low)
    def _():
        corner_down.wait_send()

    if with_corr:
        for n, src in ((6, r["sd1"]), (7, r["sd2"])):
            some = src.at[0 : count_x - 1]
            remote(some, some, n, before).wait_send()


def hand_over(final_in, corr_in, final_out, corr_out):
    final_out[...] = final_in[...]
    corr_out[...] = corr_in[...]


def per_device(run, with_corr, phase_field, solute, pull_counts, planes):
    w1, cs, back, w2 = (jnp.asarray(t) for t in tables())
    wide = 2 * TOP + NR
    vmem = lambda *shape: pltpu.VMEM(shape, F32)
    scratch = [
        vmem(NP + 4, wide, NL),
        vmem(NP + 3, wide, NL),
        vmem(NP + 4, wide, NL),
        vmem(NP + 2, NR, NL),
        vmem(18, NR, NL),
        *[vmem(3, NR, NL) for _ in range(4)],
        *[vmem(3, NP, NL) for _ in range(4)],
        *[vmem(2, NL) for _ in range(4)],
        *[pltpu.VMEM(PIECE, jnp.int32) for _ in range(3)],
        *[vmem(1, NR, NL) for _ in range(4)],
        *[vmem(32, *PIECE) for _ in range(4)],
        *[pltpu.VMEM(t.shape, BF16) for t in (w1, cs, back, w2)],
        *[
            vmem(n, 8, NL * 4 // len(seam_columns(run, kind)))
            for n, kind in zip(MESSAGES, ["small"] * 4 + ["bulk"] * 3 + ["onward"])
        ],
        pltpu.SemaphoreType.DMA((8, 4)),
        pltpu.SemaphoreType.DMA((16,)),
        pltpu.SemaphoreType.DMA((10,)),
    ]
    smem = pl.BlockSpec(memory_space=pltpu.SMEM)
    anywhere = pl.BlockSpec(memory_space=pl.ANY)
    local = pl.BlockSpec(memory_space=pltpu.VMEM)
    final, corr = pl.pallas_call(
        functools.partial(kernel, run, with_corr),
        out_shape=(
            jax.ShapeDtypeStruct((NP, NR, NL), F32),
            jax.ShapeDtypeStruct((1, NR, NL), F32),
        ),
        in_specs=[smem, smem, *[anywhere] * 6],
        out_specs=(local, local),
        scratch_shapes=scratch,
        compiler_params=pltpu.CompilerParams(
            collective_id=0, has_side_effects=True, vmem_limit_bytes=56 * 1024 * 1024
        ),
    )(pull_counts, planes, phase_field, solute, w1, cs, back, w2)
    return pl.pallas_call(
        hand_over,
        out_shape=(
            jax.ShapeDtypeStruct((NP, NR, NL), F32),
            jax.ShapeDtypeStruct((1, NR, NL), F32),
        ),
        in_specs=[local, local],
        out_specs=(local, local),
    )(final, corr)


def build(mesh, run, with_corr):
    return jax.shard_map(
        functools.partial(per_device, run, with_corr),
        mesh=mesh,
        in_specs=(P("gz", "gx", None), P("gz", "gx", None), P(), P("gz")),
        out_specs=(P("gz", "gx", None), P("gz", "gx", None)),
        check_vma=False,
    )


def solution(mesh):
    return build(mesh, RUN, True)
```

```python
import functools
import math

import jax
import jax.numpy as jnp
import ml_dtypes
import numpy as np
from jax import lax
from jax.experimental import pallas as pl
from jax.experimental.pallas import tpu as pltpu
from jax.sharding import PartitionSpec as P

MESH = pl.DeviceIdType.MESH
F32 = jnp.float32
BF16 = jnp.bfloat16

TIME_STEP = 0.05
PARTITION = 0.15
COUPLING = 1.6
DIFFUSIVITY = 0.4
FAR = -1.0

NP, NR, NL = 8, 32, 1024
HALF = NL // 2
RUN = 8
TOP = 8
PIECE = (8, 128)


def split_bf16(table):
    high = table.astype(ml_dtypes.bfloat16)
    low = (table - high.astype(np.float64)).astype(ml_dtypes.bfloat16)
    return np.stack([high, low])


@functools.lru_cache(None)
def tables():
    w = 2.0 * math.pi / NL
    parts, part_rows = 16, 32
    m = np.arange(parts)[:, None]
    l = np.arange(part_rows)[None, :]
    order = np.arange(HALF)
    near = np.arange(HALF)

    def trig(a, b):
        angle = (a[:, None] * b[None, :]) % NL
        return np.cos(w * angle), np.sin(w * angle)

    w1, w2 = [], []
    for odd in (0, 1):
        ky = np.broadcast_to(2 * (16 * m + l % 16) + odd, (parts, part_rows)).reshape(-1)
        imag = np.broadcast_to(l >= 16, (parts, part_rows)).reshape(-1)
        c, s = trig(near, ky)
        fwd = np.where(imag[None, :], -s, c)
        inv = 2.0 * np.where(imag[None, :], -s, c)
        if not odd:
            fwd[:, 16] = (-1.0) ** near
            inv[:, 0] = 1.0
            inv[:, 16] = (-1.0) ** near
        w1.append(fwd)
        inv = inv.reshape(HALF, parts, 4, 8).transpose(0, 2, 1, 3).reshape(HALF, HALF)
        w2.append(inv.T / (NL * NL * float(NL)))
    g, i, r = np.meshgrid(np.arange(4), np.arange(parts), np.arange(8), indexing="ij")
    x = (32 * i + 8 * g + r).reshape(-1)
    cs, back = [], []
    for odd in (0, 1):
        kx = 2 * order + odd
        cs.append(np.concatenate(trig(x, kx), 1))
        back.append(np.concatenate(trig(kx, near), 1))
    return tuple(split_bf16(np.stack(t)) for t in (w1, cs, back, w2))


def mm(x, table, odd):
    rows = x.shape[0]
    high = x.astype(BF16)
    low = (x - high.astype(F32)).astype(BF16)
    both = jnp.concatenate([high, low], 0)
    first = jnp.dot(both, table[0, odd], preferred_element_type=F32)
    second = jnp.dot(high, table[1, odd], preferred_element_type=F32)
    return first[:rows] + first[rows:] + second


def pack(block, out, base=0):
    lane_group = lax.broadcasted_iota(jnp.int32, PIECE, 1) // 32
    for c in range(block.shape[1] // 128):
        v = [block[8 * g : 8 * g + 8, 128 * c : 128 * c + 128] for g in range(4)]
        for b in range(4):
            tile = v[b]
            for g in range(4):
                if g != b:
                    moved = pltpu.roll(v[g], (32 * (g - b)) % 128, 1)
                    tile = jnp.where(lane_group == g, moved, tile)
            out[base + 4 * c + b] = tile


def unpack(tiles):
    flat = tiles[...].reshape(256, 128)
    turned = flat.T
    return jnp.concatenate([turned[32 * g : 32 * g + 32] for g in range(4)], 1)


def seam_columns(run, kind):
    if run < 8 or kind == "small":
        return (0, run - 1, run // 2 - 1, run // 2)
    if kind == "onward":
        return (0, 2, 3, 4)
    return (0, 7, 3, 4, 0, 5, 1, 6)


def greeting_columns(run, up):
    kinds = ("small",) if up else ("small", "onward", "bulk")
    return tuple(sorted({c for kind in kinds for c in seam_columns(run, kind)}))


class Message:
    def __init__(self, env, index, up, src, dst, kind):
        self.src, self.dst, self.up = src, dst, up
        self.sems = [env["msem"].at[index, j] for j in range(4)]
        self.relay_ref = env["ra"][index]
        self.run, self.height = env["run"], env["height"]
        self.y = (self.run - 1 - env["y"]) if up else env["y"]
        self.h = (self.height - 1 - env["h"]) if up else env["h"]
        self.columns = seam_columns(self.run, kind)
        self.width = NL * 4 // len(self.columns)

    def copy(self, src, dst, send, recv, y, h):
        if self.up:
            y, h = self.run - 1 - y, self.height - 1 - h
        return pltpu.make_async_remote_copy(
            src_ref=src,
            dst_ref=dst,
            send_sem=self.sems[send],
            recv_sem=self.sems[recv],
            device_id={"gz": h * self.run + y},
            device_id_type=MESH,
        )

    def piece(self, ref, n):
        g, part = n % 4, n // 4
        return ref.at[:, 8 * g : 8 * g + 8, self.width * part : self.width * (part + 1)]

    def relayed(self, early=None):
        pieces = [n for n, c in enumerate(self.columns) if c > 0]
        if early is None:
            return pieces
        return [n for n in pieces if (self.columns[n] == self.run - 1) == early]

    def has_target(self):
        return jnp.logical_or(self.y > 0, self.h > 0)

    def has_source(self):
        return jnp.logical_or(self.y < self.run - 1, self.h < self.height - 1)

    def start(self):
        self.start_seam(True)
        self.start_seam(False)
        self.start_inside()

    def start_inside(self):
        @pl.when(self.y > 0)
        def _():
            self.copy(self.src, self.dst, 0, 1, self.y - 1, self.h).start()

    def start_seam(self, early):
        @pl.when(jnp.logical_and(self.y == 0, self.h > 0))
        def _():
            for n in self.relayed(early):
                column = self.columns[n]
                self.copy(self.piece(self.src, n), self.relay_ref, 0, 3, column, self.h).start()
            direct = [] if early else [n for n, c in enumerate(self.columns) if c == 0]
            for n in direct:
                there = self.piece(self.dst, n)
                end = self.run - 1
                self.copy(self.piece(self.src, n), there, 0, 1, end, self.h - 1).start()

    def relay(self, early=None):
        end = self.run - 1
        for n in self.relayed(early):

            @pl.when(jnp.logical_and(self.h > 0, self.y == self.columns[n]))
            def _(n=n):
                self.copy(self.relay_ref, self.relay_ref, 2, 3, end, self.h - 1).wait_recv()
                there = self.piece(self.dst, n)
                self.copy(self.relay_ref, there, 2, 1, end, self.h - 1).start()

    def arrive(self):
        @pl.when(self.has_source())
        def _():
            self.copy(self.src, self.dst, 0, 1, 0, 0).wait_recv()

    def finish(self):
        @pl.when(self.has_target())
        def _():
            self.copy(self.src, self.dst, 0, 1, 0, 0).wait_send()

        column = [self.y == self.columns[n] for n in self.relayed()]

        @pl.when(jnp.logical_and(self.h > 0, functools.reduce(jnp.logical_or, column)))
        def _():
            self.copy(self.relay_ref, self.relay_ref, 2, 3, 0, 0).wait_send()


MESSAGES = (3, 3, 1, 1, 2, 4, 2, 2)


def lane_sides(v):
    return pltpu.roll(v, 1, 1), pltpu.roll(v, NL - 1, 1)


def driving_of(centre, total, solute_now, thermal):
    gap = 1.0 - centre * centre
    return (total - 6.0 * centre) + centre * gap - COUPLING * (gap * gap) * (solute_now + thermal)


def advance_phase(centre, driving):
    return jnp.clip(centre + TIME_STEP * driving, -1.0, 1.0)


NAMES = (
    "pulls", "plane", "phase", "solute", "w1", "cs", "back", "w2", "final", "corr", "ph", "so",
    "p1", "s1", "fb", "hsd", "hsu", "hrd", "hru", "xsl", "xsh", "xrl", "xrh", "cse", "csu",
    "cre", "cru", "ixs", "ixa", "ixb", "c2s", "c2r", "c1s", "c1r", "sd1", "rv1", "sd2", "rv2",
    "v1", "vcs", "vback", "v2",
    *["ra%d" % n for n in range(8)],
    "msem", "osem", "lsem",
)


def kernel(run, with_corr, *refs):
    r = dict(zip(NAMES, refs, strict=True))
    k = lax.axis_index("gz")
    i = lax.axis_index("gx")
    count_z, count_x = lax.axis_size("gz"), lax.axis_size("gx")
    height = count_z // run
    y, h = lax.rem(k, run), lax.div(k, run)
    at_top = k == count_z - 1
    ph, so, p1, s1, fb = (r[n] for n in ("ph", "so", "p1", "s1", "fb"))
    lsem, osem = r["lsem"], r["osem"]

    own = slice(TOP, TOP + NR)
    load_phase = pltpu.make_async_copy(r["phase"], ph.at[2 : 2 + NP, own, :], lsem.at[0])
    load_solute = pltpu.make_async_copy(r["solute"], so.at[1 : 1 + NP, own, :], lsem.at[1])
    stage = [
        pltpu.make_async_copy(r["phase"].at[0:2], r["hsd"].at[0:2], lsem.at[6]),
        pltpu.make_async_copy(r["solute"].at[0:1], r["hsd"].at[2:3], lsem.at[7]),
        pltpu.make_async_copy(r["phase"].at[NP - 2 : NP], r["hsu"].at[0:2], lsem.at[8]),
        pltpu.make_async_copy(r["solute"].at[NP - 1 : NP], r["hsu"].at[2:3], lsem.at[9]),
    ]
    loads = [
        pltpu.make_async_copy(r[a], r[b], lsem.at[2 + n])
        for n, (a, b) in enumerate((("w1", "v1"), ("cs", "vcs"), ("back", "vback"), ("w2", "v2")))
    ]
    for copy in (load_phase, load_solute, *stage, *loads):
        copy.start()

    barrier = pltpu.get_barrier_semaphore()

    def is_column(up):
        return functools.reduce(jnp.logical_or, [y == (run - 1 - c if up else c) for c in greeting_columns(run, up)])

    def greet(other):
        pl.semaphore_signal(barrier, inc=1, device_id={"gz": other}, device_id_type=MESH)

    greetings = (count_x - 1) + (run - 1)
    for up in (False, True):
        near, far = (h < height - 1, h > 0) if up else (h > 0, h < height - 1)
        step = 1 if up else -1
        last = 0 if up else run - 1

        @pl.when(jnp.logical_and(near, is_column(up)))
        def _(step=step, last=last):
            greet((h + step) * run + last)

        @pl.when(jnp.logical_and(far, y == last))
        def _(up=up, step=step):
            for c in greeting_columns(run, up):
                greet((h - step) * run + (run - 1 - c if up else c))

        greetings = greetings + jnp.where(jnp.logical_and(near, is_column(up)), 1, 0)
        greetings = greetings + jnp.where(jnp.logical_and(far, y == last), len(greeting_columns(run, up)), 0)

    def greet_y(j, carry):
        other = h * run + lax.rem(y + j, run)
        pl.semaphore_signal(barrier, inc=1, device_id={"gz": other}, device_id_type=MESH)
        return carry

    lax.fori_loop(1, run, greet_y, 0)
    def greet_x(j, carry):
        other = lax.rem(i + j, count_x)
        pl.semaphore_signal(barrier, inc=1, device_id={"gx": other}, device_id_type=MESH)
        return carry

    lax.fori_loop(1, count_x, greet_x, 0)

    load_phase.wait()
    load_solute.wait()
    for copy in stage:
        copy.wait()
    for p in range(NP):
        at = slice(p, p + 1)
        r["xsl"][0, at, :] = ph[p + 2, TOP : TOP + 1, :]
        r["xsl"][1, at, :] = ph[p + 2, TOP + 1 : TOP + 2, :]
        r["xsl"][2, at, :] = so[p + 1, TOP : TOP + 1, :]
        r["xsh"][0, at, :] = ph[p + 2, TOP + NR - 1 : TOP + NR, :]
        r["xsh"][1, at, :] = ph[p + 2, TOP + NR - 2 : TOP + NR - 1, :]
        r["xsh"][2, at, :] = so[p + 1, TOP + NR - 1 : TOP + NR, :]
    r["ixs"][...] = jnp.full(PIECE, r["plane"][0], jnp.int32)

    pl.semaphore_wait(barrier, greetings)

    env = {
        "msem": r["msem"],
        "ra": [r["ra%d" % n] for n in range(8)],
        "run": run,
        "height": height,
        "y": y,
        "h": h,
    }
    down = Message(env, 0, False, r["hsd"], r["hrd"], "small")
    upward = Message(env, 1, True, r["hsu"], r["hru"], "small")
    second = Message(env, 2, False, r["c2s"], r["c2r"], "small")
    first = Message(env, 3, False, r["c1s"], r["c1r"], "small")
    bulk = [
        Message(env, 4, False, fb.at[0:2], fb.at[8:10], "bulk"),
        Message(env, 5, False, fb.at[2:6], fb.at[10:14], "bulk"),
        Message(env, 6, False, fb.at[6:8], fb.at[14:16], "bulk"),
    ]
    onward = Message(env, 7, False, fb.at[8:10], fb.at[16:18], "onward")

    def remote(src, dst, n, target):
        return pltpu.make_async_remote_copy(
            src_ref=src,
            dst_ref=dst,
            send_sem=osem.at[2 * n],
            recv_sem=osem.at[2 * n + 1],
            device_id=target,
            device_id_type=MESH,
        )

    above = {"gz": lax.rem(k + 1, count_z)}
    below = {"gz": lax.rem(k + count_z - 1, count_z)}
    not_top = jnp.logical_not(at_top)
    not_low = k > 0

    for message in (down, upward):
        message.start_seam(False)
        message.start_seam(True)
    before = {"gx": lax.rem(i + count_x - 1, count_x)}
    after = {"gx": lax.rem(i + 1, count_x)}
    to_before = remote(r["xsl"], r["xrh"], 0, before)
    to_after = remote(r["xsh"], r["xrl"], 1, after)
    to_before.start()
    to_after.start()
    index_first = remote(r["ixs"], r["ixa"], 2, above)
    index_second = remote(r["ixa"], r["ixb"], 3, above)

    @pl.when(not_top)
    def _():
        index_first.start()

    to_before.wait_recv()
    to_after.wait_recv()
    r["cse"][0:1, :] = r["xrl"][0, 0:1, :]
    r["cse"][1:2, :] = r["xrh"][0, 0:1, :]
    r["csu"][0:1, :] = r["xrl"][0, NP - 1 : NP, :]
    r["csu"][1:2, :] = r["xrh"][0, NP - 1 : NP, :]
    corner_down = remote(r["cse"], r["cre"], 4, below)
    corner_up = remote(r["csu"], r["cru"], 5, above)

    @pl.when(not_low)
    def _():
        corner_down.start()

    @pl.when(not_top)
    def _():
        corner_up.start()

    down.relay()
    upward.relay()
    down.start_inside()
    upward.start_inside()

    for p in range(NP):
        ph[p + 2, TOP - 1 : TOP, :] = r["xrl"][0, p : p + 1, :]
        ph[p + 2, TOP + NR : TOP + NR + 1, :] = r["xrh"][0, p : p + 1, :]

    @pl.when(not_low)
    def _():
        index_first.wait_recv()

    @pl.when(jnp.logical_and(not_top, not_low))
    def _():
        index_second.start()

    pull_first = r["pulls"][0]
    pull_both = pull_first + r["pulls"][1]

    def thermal_of(plane):
        return ((2 * plane - count_z * NP).astype(F32)) * (1.0 / (count_z * NP))

    def row_groups():
        return [TOP + 8 * g for g in range(NR // 8)]

    def first_step(p, with_solute):
        thermal = thermal_of(k * NP + p - pull_first)
        for a in row_groups():
            rows = slice(a, a + 8)
            centre = ph[p + 2, rows, :]
            sides = [
                ph[p + 1, rows, :],
                ph[p + 3, rows, :],
                ph[p + 2, a - 1 : a + 7, :],
                ph[p + 2, a + 1 : a + 9, :],
                *lane_sides(centre),
            ]
            here = so[p + 1, rows, :]
            total = sum(sides)
            driving = driving_of(centre, total, here, thermal)
            p1[p + 1, rows, :] = advance_phase(centre, driving)
            if with_solute:
                solute_sides = [
                    so[p, rows, :],
                    so[p + 2, rows, :],
                    so[p + 1, a - 1 : a + 7, :],
                    so[p + 1, a + 1 : a + 9, :],
                    *lane_sides(here),
                ]
                mixed = sum(u * v for u, v in zip(sides, solute_sides))
                spread = sum(solute_sides) - 6.0 * here
                flux = 0.25 * ((2.0 - centre) * spread - mixed + here * total)
                rate = (DIFFUSIVITY * flux + 0.5 * (1.0 + (1.0 - PARTITION) * here) * driving) / (
                    0.5 * (1.0 + PARTITION) - 0.5 * (1.0 - PARTITION) * centre
                )
                s1[p, a - TOP : a - TOP + 8, :] = here + TIME_STEP * rate

    def second_step(p):
        plane = k * NP + p
        thermal = thermal_of(plane - pull_both)
        for a in row_groups():
            rows = slice(a, a + 8)
            centre = p1[p + 1, rows, :]
            low = jnp.where(plane == pull_both, centre, p1[p, rows, :])
            total = sum(
                [
                    low,
                    p1[p + 2, rows, :],
                    p1[p + 1, a - 1 : a + 7, :],
                    p1[p + 1, a + 1 : a + 9, :],
                    *lane_sides(centre),
                ]
            )
            driving = driving_of(centre, total, s1[p, a - TOP : a - TOP + 8, :], thermal)
            fb[p, a - TOP : a - TOP + 8, :] = advance_phase(centre, driving)

    def second_body(p, carry):
        second_step(p)
        return carry

    for p in range(NP):
        so[p + 1, TOP - 1 : TOP, :] = r["xrl"][2, p : p + 1, :]
        so[p + 1, TOP + NR : TOP + NR + 1, :] = r["xrh"][2, p : p + 1, :]

    def first_body(p, carry):
        first_step(p, True)
        return carry

    plane_row = lax.broadcasted_iota(jnp.int32, (NP, NL), 0)
    thermal_rows = (2 * (plane_row + (k * NP - pull_first)) - count_z * NP).astype(F32) * (
        1.0 / (count_z * NP)
    )

    def rows_beside(planes, with_ends):
        for side, (got, sent, at) in enumerate(
            ((r["xrl"], r["xsl"], TOP - 1), (r["xrh"], r["xsh"], TOP + NR))
        ):
            centre = got[0]
            low, high = pltpu.roll(centre, 1, 0), pltpu.roll(centre, NP - 1, 0)
            if with_ends:
                low = jnp.where(plane_row == 0, r["cru"][side : side + 1, :], low)
                high = jnp.where(plane_row == NP - 1, r["cre"][side : side + 1, :], high)
            total = sum([low, high, got[1], sent[0], *lane_sides(centre)])
            driving = driving_of(centre, total, got[2], thermal_rows)
            moved = advance_phase(centre, driving)
            for p in planes:
                p1[p + 1, at : at + 1, :] = moved[p : p + 1, :]

    lax.fori_loop(1, NP - 1, first_body, 0)
    rows_beside(range(1, NP - 1), False)
    lax.fori_loop(2, NP - 2, second_body, 0)

    @pl.when(at_top)
    def _():
        ph[NP + 2 : NP + 4] = jnp.full((2, 2 * TOP + NR, NL), FAR, F32)
        so[NP + 1 : NP + 3] = jnp.full((2, 2 * TOP + NR, NL), FAR, F32)
        r["cre"][...] = jnp.full((2, NL), FAR, F32)
        p1[NP + 2 : NP + 4] = jnp.full((2, 2 * TOP + NR, NL), FAR, F32)
        s1[NP + 1 : NP + 2] = jnp.full((1, NR, NL), FAR, F32)

    @pl.when(k == 0)
    def _():
        ph[0:2] = jnp.full((2, 2 * TOP + NR, NL), FAR, F32)
        so[0:1] = jnp.full((1, 2 * TOP + NR, NL), FAR, F32)
        r["cru"][...] = jnp.full((2, NL), FAR, F32)

    @pl.when(not_low)
    def _():
        corner_up.wait_recv()

    @pl.when(not_top)
    def _():
        corner_down.wait_recv()

    down.arrive()
    upward.arrive()

    @pl.when(not_top)
    def _():
        ph[NP + 2, own, :] = r["hrd"][0]
        ph[NP + 3, own, :] = r["hrd"][1]
        so[NP + 1, own, :] = r["hrd"][2]

    @pl.when(not_low)
    def _():
        ph[0, own, :] = r["hru"][0]
        ph[1, own, :] = r["hru"][1]
        so[0, own, :] = r["hru"][2]

    ph[1, TOP - 1 : TOP, :] = r["cru"][0:1, :]
    ph[1, TOP + NR : TOP + NR + 1, :] = r["cru"][1:2, :]
    ph[NP + 2, TOP - 1 : TOP, :] = r["cre"][0:1, :]
    ph[NP + 2, TOP + NR : TOP + NR + 1, :] = r["cre"][1:2, :]

    first_step(-1, False)
    first_step(0, True)
    first_step(NP - 1, True)
    rows_beside((0, NP - 1), True)

    @pl.when(not_top)
    def _():
        first_step(NP, False)

    @pl.when(at_top)
    def _():
        first_step(NP, True)
        for got, at in ((r["xrl"], TOP - 1), (r["xrh"], TOP + NR)):
            centre = jnp.full((NP, NL), FAR, F32)
            low = jnp.where(plane_row == 0, pltpu.roll(got[0], 1, 0), FAR)
            total = low + 5.0 * FAR
            driving = driving_of(centre, total, centre, 0.0)
            p1[NP + 1, at : at + 1, :] = advance_phase(centre, driving)[0:1, :]

    lax.fori_loop(0, 2, second_body, 0)

    def mask_of(which, local):
        return jnp.broadcast_to(which[0:1, 0:1] == local, (NR, NL))

    @pl.when(k == 0)
    def _():
        r["ixa"][...] = jnp.zeros(PIECE, jnp.int32)

    @pl.when(k > 1)
    def _():
        index_second.wait_recv()

    @pl.when(k <= 1)
    def _():
        r["ixb"][...] = jnp.zeros(PIECE, jnp.int32)

    two = r["ixb"][...] + (pull_both - k * NP)
    one = r["ixa"][...] + (pull_both - k * NP)
    none = r["ixs"][...] + (pull_both - k * NP)
    r["c2s"][0] = jnp.where(mask_of(two, 1), fb[1], fb[0])
    second.start()
    second.relay()
    lax.fori_loop(NP - 2, NP, second_body, 0)

    @pl.when(at_top)
    def _():
        second_step(NP)
        second_step(NP + 1)
        fb[NP + 2 : NP + 10] = jnp.full((8, NR, NL), FAR, F32)
        r["c2r"][0] = jnp.where(mask_of(one, NP), fb[NP], fb[NP + 1])
        r["c1r"][0] = jnp.where(
            mask_of(none, NP), fb[NP], jnp.where(mask_of(none, NP + 1), fb[NP + 1], FAR)
        )

    picked = fb[0]
    for p in range(1, NP):
        picked = jnp.where(mask_of(one, p), fb[p], picked)
    r["c1s"][0] = picked
    first.relay(True)
    second.arrive()
    beyond = jnp.broadcast_to(one[0:1, 0:1] >= NP, (NR, NL))
    r["c1s"][0] = jnp.where(beyond, r["c2r"][0], r["c1s"][0])
    first.start()
    for message in bulk:
        message.start_seam(True)
    for message in bulk:
        message.start_seam(False)
        message.start_inside()
    first.relay(False)
    for message in bulk:
        message.relay(True)
    first.arrive()
    inside = jnp.broadcast_to(none[0:1, 0:1] < NP, (NR, NL))
    section = jnp.where(
        inside, jnp.where(mask_of(none, NP - 1), fb[NP - 1], fb[NP - 2]), r["c1r"][0]
    )

    for load in loads:
        load.wait()

    def send_tiles(src, dst, n, first, count):
        def one_copy(j, carry):
            other = first + lax.rem(i + j, count)

            @pl.when(other != i)
            def _():
                remote(src.at[other], dst.at[i], n, {"gx": other}).start()

            return carry

        lax.fori_loop(1, count + 1, one_copy, 0)

    def await_tiles(src, dst, n):
        dst[i] = src[i]
        some = slice(0, count_x - 1)
        remote(src.at[some], dst.at[some], n, before).wait_recv()

    row_sum = jnp.sum(section, axis=1, keepdims=True)
    level = section - row_sum * (1.0 / NL)
    near, far = level[:, :HALF], level[:, HALF:]
    half = max(count_x // 2, 1)
    even = mm(near + far, r["v1"], 0)
    lane = lax.broadcasted_iota(jnp.int32, (NR, HALF), 1)
    pack(jnp.where(lane == 0, row_sum, even), r["sd1"])
    if with_corr:
        send_tiles(r["sd1"], r["rv1"], 6, 0, half)
    pack(mm(near - far, r["v1"], 1), r["sd1"], half)
    if with_corr:
        send_tiles(r["sd1"], r["rv1"], 6, half, half)
    for message in bulk:
        message.relay(False)

    @pl.when(y == 0)
    def _():
        bulk[0].arrive()

    onward.start_seam(True)
    onward.start_seam(False)

    if with_corr:
        await_tiles(r["sd1"], r["rv1"], 6)

        rows = unpack(r["rv1"])
        row = lax.broadcasted_iota(jnp.int32, (NR, NL), 0)
        lowest = jnp.logical_and(row == 0, jnp.broadcast_to(i, (NR, NL)) == 0)
        mean = jnp.sum(rows, axis=1, keepdims=True) * (1.0 / NL)
        rows = jnp.where(lowest, rows - mean, rows)
        starts = [256 * g for g in range(4)]
        near = jnp.concatenate([rows[:, s : s + 128] for s in starts], 1)
        far = jnp.concatenate([rows[:, s + 128 : s + 256] for s in starts], 1)
        special_row = jnp.logical_and(
            lax.broadcasted_iota(jnp.int32, (16, HALF), 0) == 0,
            jnp.broadcast_to(i, (16, HALF)) == 0,
        )
        first_lane = lax.broadcasted_iota(jnp.int32, (16, HALF), 1) == 0
        halves = []
        for odd, part in enumerate((near + far, near - far)):
            z = mm(part, r["vcs"], odd)
            ac, as_ = z[:16, :HALF], z[:16, HALF:]
            bc, bs = z[16:, :HALF], z[16:, HALF:]
            real, imag = ac + bs, bc - as_
            power = real * real + imag * imag
            lone = ac * ac + as_ * as_
            if not odd:
                lone = jnp.where(first_lane, 0.0, lone)
            power = jnp.where(special_row, lone, power)
            halves.append(mm(jnp.concatenate([power, bc * bc + bs * bs], 0), r["vback"], odd))
        even, odd_part = halves
        lags = jnp.concatenate(
            [
                even[:, :HALF] + odd_part[:, :HALF],
                even[:, :HALF] - odd_part[:, :HALF],
            ],
            1,
        )
        sines = jnp.concatenate(
            [
                even[:16, HALF:] + odd_part[:16, HALF:],
                even[:16, HALF:] - odd_part[:16, HALF:],
            ],
            1,
        )
        special_wide = jnp.logical_and(
            lax.broadcasted_iota(jnp.int32, (16, NL), 0) == 0,
            jnp.broadcast_to(i, (16, NL)) == 0,
        )
        sines = jnp.where(special_wide, lags[16:], sines)
        pack(jnp.concatenate([lags[:16], sines], 0), r["sd2"])
        send_tiles(r["sd2"], r["rv2"], 7, 0, count_x)
    onward.relay()

    @pl.when(y > 0)
    def _():
        bulk[0].arrive()
        onward.start_inside()

    if with_corr:
        await_tiles(r["sd2"], r["rv2"], 7)
        rows = unpack(r["rv2"])
        even = jnp.concatenate([rows[:, s : s + 128] for s in starts], 1)
        odd_part = jnp.concatenate([rows[:, s + 128 : s + 256] for s in starts], 1)
        even = mm(even, r["v2"], 0)
        odd_part = mm(odd_part, r["v2"], 1)
        r["corr"][0, :, :HALF] = even + odd_part
        r["corr"][0, :, HALF:] = even - odd_part
    else:
        r["corr"][0] = section
    bulk[1].arrive()
    bulk[2].arrive()
    onward.arrive()
    r["final"][...] = fb[pl.ds(pull_both, NP)]

    for message in (down, upward, second, first, *bulk, onward):
        message.finish()
    to_before.wait_send()
    to_after.wait_send()

    @pl.when(not_top)
    def _():
        index_first.wait_send()
        corner_up.wait_send()

    @pl.when(jnp.logical_and(not_top, not_low))
    def _():
        index_second.wait_send()

    @pl.when(not_low)
    def _():
        corner_down.wait_send()

    if with_corr:
        for n, src in ((6, r["sd1"]), (7, r["sd2"])):
            some = src.at[0 : count_x - 1]
            remote(some, some, n, before).wait_send()


def hand_over(final_in, corr_in, final_out, corr_out):
    final_out[...] = final_in[...]
    corr_out[...] = corr_in[...]


def per_device(run, with_corr, phase_field, solute, pull_counts, planes):
    w1, cs, back, w2 = (jnp.asarray(t) for t in tables())
    wide = 2 * TOP + NR
    vmem = lambda *shape: pltpu.VMEM(shape, F32)
    scratch = [
        vmem(NP + 4, wide, NL),
        vmem(NP + 3, wide, NL),
        vmem(NP + 4, wide, NL),
        vmem(NP + 2, NR, NL),
        vmem(18, NR, NL),
        *[vmem(3, NR, NL) for _ in range(4)],
        *[vmem(3, NP, NL) for _ in range(4)],
        *[vmem(2, NL) for _ in range(4)],
        *[pltpu.VMEM(PIECE, jnp.int32) for _ in range(3)],
        *[vmem(1, NR, NL) for _ in range(4)],
        *[vmem(32, *PIECE) for _ in range(4)],
        *[pltpu.VMEM(t.shape, BF16) for t in (w1, cs, back, w2)],
        *[
            vmem(n, 8, NL * 4 // len(seam_columns(run, kind)))
            for n, kind in zip(MESSAGES, ["small"] * 4 + ["bulk"] * 3 + ["onward"])
        ],
        pltpu.SemaphoreType.DMA((8, 4)),
        pltpu.SemaphoreType.DMA((16,)),
        pltpu.SemaphoreType.DMA((10,)),
    ]
    smem = pl.BlockSpec(memory_space=pltpu.SMEM)
    anywhere = pl.BlockSpec(memory_space=pl.ANY)
    local = pl.BlockSpec(memory_space=pltpu.VMEM)
    final, corr = pl.pallas_call(
        functools.partial(kernel, run, with_corr),
        out_shape=(
            jax.ShapeDtypeStruct((NP, NR, NL), F32),
            jax.ShapeDtypeStruct((1, NR, NL), F32),
        ),
        in_specs=[smem, smem, *[anywhere] * 6],
        out_specs=(local, local),
        scratch_shapes=scratch,
        compiler_params=pltpu.CompilerParams(
            collective_id=0, has_side_effects=True, vmem_limit_bytes=56 * 1024 * 1024
        ),
    )(pull_counts, planes, phase_field, solute, w1, cs, back, w2)
    return pl.pallas_call(
        hand_over,
        out_shape=(
            jax.ShapeDtypeStruct((NP, NR, NL), F32),
            jax.ShapeDtypeStruct((1, NR, NL), F32),
        ),
        in_specs=[local, local],
        out_specs=(local, local),
    )(final, corr)


def build(mesh, run, with_corr):
    return jax.shard_map(
        functools.partial(per_device, run, with_corr),
        mesh=mesh,
        in_specs=(P("gz", "gx", None), P("gz", "gx", None), P(), P("gz")),
        out_specs=(P("gz", "gx", None), P("gz", "gx", None)),
        check_vma=False,
    )


def solution(mesh):
    return build(mesh, RUN, True)
```
